128 devices in a mesh: band: 4 (over y_hi, core), space: 32 (over z, y_lo, x).
Axes of the slice: x: 4, y: 4 (y_hi: 2, y_lo: 2; y = y_hi * 2 + y_lo), z: 4, core: 2. Of those that a mesh axis runs over, the one named last changes fastest.
Arguments:
- orbitals: float32 [4, 32, 24, 192, 128], P('band', 'space'), may hold values from -3200 to 3200
- potential: float32 [32, 24, 192, 128], P('space'), may hold values from -0.5 to 0.5
Outputs:
- filtered: float32 [4, 32, 24, 192, 128], P('band', 'space')
- correlation: float32 [4, 4], replicated
The draws below stay inside these ranges and needn't reach their ends.
All inputs are finite; a program needn't handle non-finite values.
Results may differ from the reference program's by a relative error of at most 0.00095.
Values sent between devices are 32-bit elements; how exact they have to be, the bound alone decides.
No kernel may reach another device: no remote copies, remote signals or barrier semaphores. Data moves between devices by JAX's collectives and lax.ppermute only.
A program may use at most 64 MiB of HBM per device.

```python
import math
import jax
import jax.numpy as jnp
from jax import lax

BX = 24
BY = 192
BZ = 128
DOMAINS = 32
NORB = 4
NX = 192


wave_number = 1.6432


wave_height = 8.0


def draw_orbitals(key, part):
    key = jax.random.fold_in(key, 1)
    first_key = jax.random.fold_in(key, 0)
    second_key = jax.random.fold_in(key, 1)
    third_key = jax.random.fold_in(key, 2)
    seventh_key = jax.random.fold_in(key, 6)
    array_shape = (NORB, DOMAINS, BX, BY, BZ)
    orbital_scale = 0.3 * jnp.exp(jax.random.uniform(first_key, (NORB, 1, 1, 1, 1), jnp.float32, 0.0, math.log(10.0)))
    domain_index = jnp.arange(DOMAINS)
    plane_index = (domain_index // 4)[:, None] * BX + jnp.arange(BX)[None, :]
    planes = plane_index.astype(jnp.float32) / NX - 0.5
    smooth_env = (10.0 ** planes).reshape(1, DOMAINS, BX, 1, 1)
    rough_factor = jax.random.uniform(second_key, (1, DOMAINS, BX, 1, 1), jnp.float32, 0.7, 1.4)
    row_index = plane_index.reshape(DOMAINS, BX, 1, 1)
    column_index = (domain_index // 2 % 2 * BY).reshape(DOMAINS, 1, 1, 1) + jnp.arange(BY).reshape(1, 1, BY, 1)
    depth_index = (domain_index % 2 * BZ).reshape(DOMAINS, 1, 1, 1) + jnp.arange(BZ).reshape(1, 1, 1, BZ)
    offsets = (row_index + column_index + depth_index).astype(jnp.float32)
    phases = jax.random.uniform(seventh_key, (NORB, 1, 1, 1, 1), jnp.float32, 0.0, 2.0 * math.pi)
    wave_part = jnp.cos(wave_number * offsets[None] + phases)
    noise_part = jnp.clip(jax.random.normal(third_key, array_shape, jnp.float32), -6.0, 6.0)
    mixed = wave_height * wave_part + rough_factor * noise_part
    return (orbital_scale * smooth_env * mixed).astype(jnp.float32)


def steps_of(key, dims, cuts, low, top_value):
    factor_of, own = 1.0, jax.random.fold_in(key, 6)
    for position, parts in cuts:
        draws = jnp.exp(jax.random.uniform(jax.random.fold_in(own, position), (parts,), jnp.float32, low / len(cuts), top_value / len(cuts)))
        factor_of = factor_of * jnp.repeat(draws, dims[position] // parts).reshape([-1 if axis == position else 1 for axis in range(len(dims))])
    return factor_of


def setup_inputs(seed: int = 0) -> dict:
    key_list = jax.random.split(jax.random.key(seed), 3)
    return {
        "orbitals": draw_orbitals(jax.random.fold_in(key_list[2], 71), 0),
        "potential": jnp.clip(jax.random.uniform(key_list[1], (DOMAINS, BX, BY, BZ), jnp.float32, -0.5, 0.5) * steps_of(key_list[1], (DOMAINS, BX, BY, BZ), ((0, 32),), -0.4, 0.0), -0.5, 0.5),
    }


def stencil_weights():
    weights = []
    for offset in range(1, 7):
        value = 2.0 * ((-1.0) ** (offset + 1)) * math.factorial(6) ** 2 / (offset * offset * math.factorial(6 - offset) * math.factorial(6 + offset))
        weights.append(value)
    return [-2.0 * sum(weights)] + weights


def to_grid(blocks):
    leading = blocks.shape[0]
    across = DOMAINS // 4
    arranged = blocks.reshape(leading, across, 2, 2, BX, BY, BZ).transpose(0, 1, 4, 2, 5, 3, 6)
    return arranged.reshape(leading, across * BX, 2 * BY, 2 * BZ)


def to_blocks(whole_grid):
    leading = whole_grid.shape[0]
    across = DOMAINS // 4
    arranged = whole_grid.reshape(leading, across, BX, 2, BY, 2, BZ).transpose(0, 1, 3, 5, 2, 4, 6)
    return arranged.reshape(leading, DOMAINS, BX, BY, BZ)


def hamiltonian(source, potential_grid):
    weights = stencil_weights()
    summed_terms = 3.0 * weights[0] * source
    for offset in range(1, 7):
        beside_all = jnp.roll(source, offset, 0) + jnp.roll(source, -offset, 0)
        beside_all = beside_all + jnp.roll(source, offset, 1) + jnp.roll(source, -offset, 1)
        beside_all = beside_all + jnp.roll(source, offset, 2) + jnp.roll(source, -offset, 2)
        summed_terms = summed_terms + weights[offset] * beside_all
    return -0.5 * summed_terms + potential_grid * source


def reference(orbitals, potential):
    orbital_grid = to_grid(orbitals)
    potential_grid = to_grid(potential[None])[0]

    def filter_one(source):
        first_step = (hamiltonian(source, potential_grid) - 9.0 * source) / 7.0
        return 2.0 * (hamiltonian(first_step, potential_grid) - 9.0 * first_step) / 7.0 - source

    filtered_grid = lax.map(filter_one, orbital_grid)
    flat_rows = filtered_grid.reshape(filtered_grid.shape[0], -1)
    correlation = jnp.dot(flat_rows, flat_rows.T, precision=lax.Precision.HIGHEST, preferred_element_type=jnp.float32)
    cell_count = flat_rows.shape[1]
    return to_blocks(filtered_grid), correlation / jnp.float32(cell_count)
```

```python
import functools
import math

import jax
import jax.numpy as jnp
import ml_dtypes
import numpy as np
from jax import lax
from jax.experimental import pallas as pl
from jax.experimental.pallas import tpu as pltpu
from jax.sharding import PartitionSpec as P

REACH = 6
ROWS = 24
LANES = 128
SLOT = 16


def stencil_weights():
    weights = []
    for offset in range(1, 7):
        value = (
            2.0
            * (-1.0) ** (offset + 1)
            * math.factorial(6) ** 2
            / (offset * offset * math.factorial(6 - offset) * math.factorial(6 + offset))
        )
        weights.append(value)
    return [-2.0 * sum(weights)] + weights


WEIGHTS = stencil_weights()
CENTER = (-1.5 * WEIGHTS[0] - 9.0) / 7.0
SIDE = [0.0] + [-0.5 * w / 7.0 for w in WEIGHTS[1:]]


def side_weight(distance):
    distance = abs(distance)
    return SIDE[distance] if 1 <= distance <= REACH else 0.0


def z_matrices(groups):
    whole = np.zeros((groups, 2 * LANES, LANES))
    for z in range(LANES):
        for other in range(max(0, z - REACH), min(LANES, z + REACH + 1)):
            whole[:, other, z] = side_weight(other - z)
        for c in range(2 * REACH):
            position = LANES + c if c < REACH else c - 2 * REACH
            for group in range(groups):
                whole[group, LANES + SLOT * group + c, z] = side_weight(position - z)
    high = whole.astype(ml_dtypes.bfloat16)
    low = (whole - high.astype(np.float64)).astype(ml_dtypes.bfloat16)
    return high, low


def selection(groups):
    chosen = np.zeros((groups, 2 * LANES, LANES), ml_dtypes.bfloat16)
    for group in range(groups):
        for c in range(2 * REACH):
            lane = c if c < REACH else LANES - 2 * REACH + c
            chosen[group, lane, SLOT * group + c] = 1
            chosen[group, LANES + lane, SLOT * group + c] = 1
    return chosen


def split(values):
    high = values.astype(jnp.bfloat16)
    low = (values - high.astype(jnp.float32)).astype(jnp.bfloat16)
    return high, low


def pack_kernel(counts, *refs):
    pieces, choose_ref, y_ref, z_ref = refs[: len(counts)], refs[-3], refs[-2], refs[-1]
    rows = pieces[0].shape[1]
    at = 0
    for count, piece in zip(counts, pieces):
        y_ref[at : at + count, 0:8, :] = piece[:, 0:8, :]
        y_ref[at : at + count, 8:16, :] = piece[:, rows - 8 : rows, :]
        total = None
        for group in range(rows // ROWS):
            block = piece[:, group * ROWS : (group + 1) * ROWS, :].reshape(count * ROWS, LANES)
            high, low = split(block)
            part = jnp.dot(
                jnp.concatenate([high, low], axis=1),
                choose_ref[group],
                preferred_element_type=jnp.float32,
            )
            total = part if total is None else total + part
        z_ref[at : at + count, :, :] = total.reshape(count, ROWS, LANES)
        at += count


def pack_faces(pieces):
    counts = [piece.shape[0] for piece in pieces]
    planes, rows = sum(counts), pieces[0].shape[1]
    groups = rows // ROWS
    return pl.pallas_call(
        functools.partial(pack_kernel, counts),
        out_shape=(
            jax.ShapeDtypeStruct((planes, 16, LANES), jnp.float32),
            jax.ShapeDtypeStruct((planes, ROWS, LANES), jnp.float32),
        ),
        in_specs=[pl.BlockSpec(memory_space=pltpu.VMEM)] * (len(pieces) + 1),
        out_specs=(pl.BlockSpec(memory_space=pltpu.VMEM),) * 2,
        compiler_params=pltpu.CompilerParams(vmem_limit_bytes=32 << 20),
        cost_estimate=pl.CostEstimate(
            flops=planes * rows * LANES * 4, bytes_accessed=planes * rows * LANES * 4, transcendentals=0
        ),
        name="pack_faces",
    )(*pieces, jnp.asarray(selection(groups)))


def stencil_kernel(counts, second, groups, band_ref, *refs):
    n = len(counts)
    current, before, after = refs[:n], refs[n : 2 * n], refs[2 * n : 3 * n]
    y_ref, z_ref, potential_ref, high_ref, low_ref, halo_ref = refs[3 * n : 3 * n + 6]
    rest = list(refs[3 * n + 6 :])
    planes = sum(counts)
    source_ref = rest.pop(0) if second else None
    extended, gathered = rest[-2:]
    outputs = rest[:-2]
    step = pl.program_id(0)
    group = step ^ (2 * band_ref[0]) if second else step
    at = 0
    for index, count in enumerate(counts):
        here = slice(at, at + count)
        extended[here, 8 : 8 + ROWS, :] = current[index][...]
        extended[here, 0:8, :] = jnp.where(group == 0, y_ref[here, 8:16, :], before[index][...])
        extended[here, 8 + ROWS : 16 + ROWS, :] = jnp.where(
            group == groups - 1, y_ref[here, 0:8, :], after[index][...]
        )
        at += count
    own_high, own_low = split(extended[:, 8 : 8 + ROWS, :].reshape(planes * ROWS, LANES))
    face_high, face_low = split(z_ref[...].reshape(planes * ROWS, LANES))
    both_high = jnp.concatenate([own_high, face_high], axis=1)
    both_low = jnp.concatenate([own_low, face_low], axis=1)
    weights_high, weights_low = high_ref[0], low_ref[0]
    along_z = jnp.dot(both_high, weights_high, preferred_element_type=jnp.float32)
    along_z += jnp.dot(both_low, weights_high, preferred_element_type=jnp.float32)
    along_z += jnp.dot(both_high, weights_low, preferred_element_type=jnp.float32)
    gathered[...] = along_z.reshape(planes, ROWS, LANES)
    for tile in range(ROWS // 8):
        top = 8 + 8 * tile
        within = slice(8 * tile, 8 * tile + 8)
        own = [extended[p, top : top + 8, :] for p in range(planes)]
        for p in range(planes):
            total = gathered[p, within, :] + (CENTER + potential_ref[p, within, :] * (1.0 / 7.0)) * own[p]
            for k in range(1, REACH + 1):
                beside = extended[p, top + k : top + k + 8, :] + extended[p, top - k : top - k + 8, :]
                if p - k >= 0:
                    beside = beside + own[p - k]
                elif not second:
                    beside = beside + halo_ref[REACH + p - k, within, :]
                if p + k < planes:
                    beside = beside + own[p + k]
                elif second:
                    beside = beside + halo_ref[p + k - planes, within, :]
                total = total + SIDE[k] * beside
            if not second:
                target, q = (outputs[0], p) if p < planes - REACH else (outputs[1], p - planes + REACH)
                target[q, within, :] = total
            else:
                outputs[0][p, within, :] = 2.0 * total - source_ref[p, within, :]
    if second:
        for slot in range(4):

            @pl.when(step // 2 == slot)
            def _(slot=slot):
                half = pl.ds(pl.multiple_of((step % 2) * ROWS, 8), ROWS)
                outputs[1 + slot][:, half, :] = outputs[0][REACH:planes, :, :]


def apply_stencil(pieces, faces, potential, halo, band, source=None):
    second = source is not None
    counts = [piece.shape[0] for piece in pieces]
    planes, rows = sum(counts), pieces[0].shape[1]
    groups = rows // ROWS
    per = ROWS // 8
    y_faces, z_faces = faces

    def group_of(step, s):
        return step ^ (2 * s[0]) if second else step

    def now(step, s):
        return (0, group_of(step, s), 0)

    def previous(step, s):
        return (0, jnp.maximum(per * group_of(step, s) - 1, 0), 0)

    def following(step, s):
        return (0, jnp.minimum(per * group_of(step, s) + per, per * groups - 1), 0)

    def fixed(step, s):
        return (0, 0, 0)

    def weights_at(step, s):
        return (group_of(step, s), 0, 0)

    in_specs = [pl.BlockSpec((count, ROWS, LANES), now) for count in counts]
    in_specs += [pl.BlockSpec((count, 8, LANES), previous) for count in counts]
    in_specs += [pl.BlockSpec((count, 8, LANES), following) for count in counts]
    in_specs += [
        pl.BlockSpec((planes, 16, LANES), fixed),
        pl.BlockSpec((planes, ROWS, LANES), fixed),
        pl.BlockSpec((planes, ROWS, LANES), now),
        pl.BlockSpec((1, 2 * LANES, LANES), weights_at),
        pl.BlockSpec((1, 2 * LANES, LANES), weights_at),
        pl.BlockSpec((REACH, ROWS, LANES), now),
    ]
    high, low = z_matrices(groups)
    operands = list(pieces) * 3 + [y_faces, z_faces, potential, jnp.asarray(high), jnp.asarray(low), halo]
    if second:
        in_specs.append(pl.BlockSpec((planes, ROWS, LANES), now))
        operands.append(source)
        out_shape = [jax.ShapeDtypeStruct((planes, rows, LANES), jnp.float32)]
        out_specs = [pl.BlockSpec((planes, ROWS, LANES), now)]
        for _ in range(4):
            out_shape.append(jax.ShapeDtypeStruct((planes - REACH, rows // 4, LANES), jnp.float32))
            out_specs.append(pl.BlockSpec((planes - REACH, rows // 4, LANES), fixed))
    else:
        out_shape = [
            jax.ShapeDtypeStruct((planes - REACH, rows, LANES), jnp.float32),
            jax.ShapeDtypeStruct((REACH, rows, LANES), jnp.float32),
        ]
        out_specs = [
            pl.BlockSpec((planes - REACH, ROWS, LANES), now),
            pl.BlockSpec((REACH, ROWS, LANES), now),
        ]
    cells = planes * rows * LANES
    return pl.pallas_call(
        functools.partial(stencil_kernel, counts, second, groups),
        out_shape=out_shape,
        grid_spec=pltpu.PrefetchScalarGridSpec(
            num_scalar_prefetch=1,
            grid=(groups,),
            in_specs=in_specs,
            out_specs=out_specs,
            scratch_shapes=[
                pltpu.VMEM((planes, ROWS + 16, LANES), jnp.float32),
                pltpu.VMEM((planes, ROWS, LANES), jnp.float32),
            ],
        ),
        compiler_params=pltpu.CompilerParams(
            vmem_limit_bytes=40 << 20, dimension_semantics=("arbitrary",)
        ),
        cost_estimate=pl.CostEstimate(flops=cells * 60, bytes_accessed=cells * 16, transcendentals=0),
        name="second_step" if second else "first_step",
    )(band, *operands)


def halo_terms(partial_ref, halo_ref, high_side, factor, planes):
    done = []
    for j in range(planes):
        total = partial_ref[j]
        for k in range(1, REACH + 1):
            m = j + k - REACH if high_side else REACH + j - k
            if 0 <= m < REACH:
                total = total + (factor * SIDE[k]) * halo_ref[m]
        done.append(total)
    return done


def high_side_kernel(partial_ref, halo_ref, out_ref):
    for j, total in enumerate(halo_terms(partial_ref, halo_ref, True, 1.0, REACH)):
        out_ref[j] = total


def finish_first(partial, halo):
    rows = partial.shape[1]
    block = pl.BlockSpec((REACH, rows // 4, LANES), lambda step: (0, step, 0))
    cells = REACH * rows * LANES
    return pl.pallas_call(
        high_side_kernel,
        out_shape=jax.ShapeDtypeStruct(partial.shape, jnp.float32),
        grid=(4,),
        in_specs=[block, block],
        out_specs=block,
        cost_estimate=pl.CostEstimate(flops=cells * 8, bytes_accessed=cells * 12, transcendentals=0),
        name="finish_first",
    )(partial, halo)


def low_side_kernel(band_ref, partial_ref, halo_ref, out_ref, *slots):
    step = pl.program_id(0)
    for j, total in enumerate(halo_terms(partial_ref, halo_ref, False, 2.0, REACH)):
        out_ref[j] = total
    for slot in range(4):

        @pl.when(step == slot)
        def _(slot=slot):
            slots[slot][...] = out_ref[...]


def finish_filtered(filtered, halo, band):
    rows = filtered.shape[1]
    part = (REACH, rows // 4, LANES)
    block = pl.BlockSpec(part, lambda step, s: (0, step ^ s[0], 0))
    whole = pl.BlockSpec(part, lambda step, s: (0, 0, 0))
    cells = REACH * rows * LANES
    return pl.pallas_call(
        low_side_kernel,
        out_shape=[jax.ShapeDtypeStruct(filtered.shape, jnp.float32)]
        + [jax.ShapeDtypeStruct(part, jnp.float32)] * 4,
        grid_spec=pltpu.PrefetchScalarGridSpec(
            num_scalar_prefetch=1,
            grid=(4,),
            in_specs=[block, block],
            out_specs=[block] + [whole] * 4,
        ),
        input_output_aliases={1: 0},
        cost_estimate=pl.CostEstimate(flops=cells * 8, bytes_accessed=cells * 16, transcendentals=0),
        name="finish_filtered",
    )(band, filtered, halo)


PAIRS = [(i, j) for i in range(4) for j in range(i, 4)]


def add_products(refs, totals):
    planes, rows = refs[0].shape[0], refs[0].shape[1]

    def body(p, carried):
        carried = list(carried)
        for tile in range(rows // 8):
            values = [ref[p, 8 * tile : 8 * tile + 8, :] for ref in refs]
            for n, (i, j) in enumerate(PAIRS):
                carried[n] = carried[n] + values[i] * values[j]
        return tuple(carried)

    return lax.fori_loop(0, planes, body, tuple(totals))


def early_gram_kernel(*refs):
    out_ref = refs[-1]
    totals = add_products(refs[:4], [jnp.zeros((8, LANES), jnp.float32)] * len(PAIRS))
    for n in range(len(PAIRS)):
        out_ref[n] = totals[n]


def early_gram(parts):
    cells = parts[0].size
    return pl.pallas_call(
        early_gram_kernel,
        out_shape=jax.ShapeDtypeStruct((len(PAIRS), 8, LANES), jnp.float32),
        in_specs=[pl.BlockSpec(memory_space=pltpu.VMEM)] * 4,
        out_specs=pl.BlockSpec(memory_space=pltpu.VMEM),
        compiler_params=pltpu.CompilerParams(vmem_limit_bytes=16 << 20),
        cost_estimate=pl.CostEstimate(flops=cells * 20, bytes_accessed=cells * 16, transcendentals=0),
        name="early_gram",
    )(*parts)


def late_gram_kernel(band_ref, before_ref, *refs):
    out_ref = refs[-1]
    totals = add_products(refs[:4], [before_ref[n] for n in range(len(PAIRS))])
    band = band_ref[0]
    lane = lax.broadcasted_iota(jnp.int32, (1, LANES), 1)
    row = jnp.zeros((1, LANES), jnp.float32)
    for n, (i, j) in enumerate(PAIRS):
        value = jnp.sum(totals[n])
        first, other = band ^ i, band ^ j
        hit = (lane == 4 * first + other) | (lane == 4 * other + first)
        row = row + jnp.where(hit, value, 0.0)
    out_ref[...] = jnp.broadcast_to(row, out_ref.shape)


def late_gram(before, parts, band, peers):
    cells = parts[0].size
    return pl.pallas_call(
        late_gram_kernel,
        out_shape=jax.ShapeDtypeStruct((peers, LANES), jnp.float32),
        in_specs=[pl.BlockSpec(memory_space=pltpu.SMEM)] + [pl.BlockSpec(memory_space=pltpu.VMEM)] * 5,
        out_specs=pl.BlockSpec(memory_space=pltpu.VMEM),
        compiler_params=pltpu.CompilerParams(vmem_limit_bytes=16 << 20),
        cost_estimate=pl.CostEstimate(flops=cells * 20, bytes_accessed=cells * 16, transcendentals=0),
        name="late_gram",
    )(band, before, *parts)


def shifted(array, by):
    peers = lax.axis_size("space")
    return lax.ppermute(array, "space", [(i, (i + by) % peers) for i in range(peers)])


def swapped(array, axis, bit):
    return lax.ppermute(array, axis, [(i, i ^ bit) for i in range(lax.axis_size(axis))])


def band_exchange(slots):
    return [slots[0]] + [swapped(slots[k], "band", k) for k in (1, 2, 3)]


def on_device(orbitals, potential):
    source, local_potential = orbitals[0, 0], potential[0]
    planes = source.shape[0]
    band = lax.axis_index("band").astype(jnp.int32).reshape(1)
    below = shifted(source[planes - REACH :], 4)
    above = shifted(source[:REACH], -4)
    y_faces, z_faces = pack_faces([source])
    faces = swapped(y_faces, "space", 2), swapped(z_faces, "space", 1)
    first_main, first_top = apply_stencil([source], faces, local_potential, below, band)
    above_first = shifted(first_main[:REACH], -4)
    first_top = finish_first(first_top, above)
    below_first = shifted(first_top, 4)
    y_faces, z_faces = pack_faces([first_main, first_top])
    faces = swapped(y_faces, "space", 2), swapped(z_faces, "space", 1)
    filtered, *slots = apply_stencil(
        [first_main, first_top], faces, local_potential, above_first, band, source
    )
    early = early_gram(band_exchange(slots))
    filtered, *slots = finish_filtered(filtered, below_first, band)
    both = ("band", "space")
    peers = lax.axis_size(both)
    rows = late_gram(early, band_exchange(slots), band, peers)
    everyone = lax.all_to_all(rows, both, 0, 0, tiled=True)
    summed = jnp.sum(everyone, axis=0)[:16].reshape(4, 4)
    cell_count = filtered.size * lax.axis_size("space")
    return filtered[None, None], summed / jnp.float32(cell_count)


def solution(mesh):
    placed = (P("band", "space", None, None, None), P("space", None, None, None))
    return jax.shard_map(
        on_device,
        mesh=mesh,
        in_specs=placed,
        out_specs=(P("band", "space", None, None, None), P()),
        check_vma=False,
    )
```

```python
import functools
import math

import jax
import jax.numpy as jnp
import ml_dtypes
import numpy as np
from jax import lax
from jax.experimental import pallas as pl
from jax.experimental.pallas import tpu as pltpu
from jax.sharding import PartitionSpec as P

REACH = 6
ROWS = 24
LANES = 128
VMEM_LIMIT = 12 << 20
VMEM = pl.BlockSpec(memory_space=pltpu.VMEM)
SMEM = pl.BlockSpec(memory_space=pltpu.SMEM)
ANY = pl.BlockSpec(memory_space=pl.ANY)
HBM = pl.BlockSpec(memory_space=pltpu.HBM)
COST = pl.CostEstimate(flops=1, bytes_accessed=1, transcendentals=0)
SLOT = 16


def stencil_weights():
    weights = []
    for offset in range(1, 7):
        value = (
            2.0
            * (-1.0) ** (offset + 1)
            * math.factorial(6) ** 2
            / (offset * offset * math.factorial(6 - offset) * math.factorial(6 + offset))
        )
        weights.append(value)
    return [-2.0 * sum(weights)] + weights


WEIGHTS = stencil_weights()
CENTER = (-1.5 * WEIGHTS[0] - 9.0) / 7.0
SIDE = [0.0] + [-0.5 * w / 7.0 for w in WEIGHTS[1:]]


def side_weight(distance):
    distance = abs(distance)
    return SIDE[distance] if 1 <= distance <= REACH else 0.0


def z_matrix():
    whole = np.zeros((2 * LANES, LANES))
    for z in range(LANES):
        for other in range(max(0, z - REACH), min(LANES, z + REACH + 1)):
            whole[other, z] = side_weight(other - z)
        for c in range(2 * REACH):
            position = LANES + c if c < REACH else c - 2 * REACH
            whole[LANES + c, z] = side_weight(position - z)
    high = whole.astype(ml_dtypes.bfloat16)
    low = (whole - high.astype(np.float64)).astype(ml_dtypes.bfloat16)
    return np.concatenate([high, low], axis=1)


def selection(group):
    lane = lax.broadcasted_iota(jnp.int32, (LANES, LANES), 0)
    slot = lax.broadcasted_iota(jnp.int32, (LANES, LANES), 1) - SLOT * group
    low = (slot >= 0) & (slot < REACH) & (lane == slot)
    high = (slot >= REACH) & (slot < 2 * REACH) & (lane == slot + (LANES - 2 * REACH))
    chosen = jnp.where(low | high, 1.0, 0.0).astype(jnp.bfloat16)
    return jnp.concatenate([chosen, chosen], axis=0)


def split(values):
    high = values.astype(jnp.bfloat16)
    low = (values - high.astype(jnp.float32)).astype(jnp.bfloat16)
    return high, low


def pack_into(pieces, y_ref, z_ref):
    at = 0
    for piece in pieces:
        count, rows = piece.shape[0], piece.shape[1]
        for p in range(count):
            base = 2 * REACH * (at + p)
            y_ref[base : base + REACH, :] = piece[p, 0:REACH, :]
            y_ref[base + REACH : base + 2 * REACH, :] = piece[p, rows - REACH : rows, :]
        total = None
        for group in range(rows // ROWS):
            block = piece[:, group * ROWS : (group + 1) * ROWS, :].reshape(count * ROWS, LANES)
            high, low = split(block)
            part = jnp.dot(
                jnp.concatenate([high, low], axis=1),
                selection(group),
                preferred_element_type=jnp.float32,
            )
            total = part if total is None else total + part
        z_ref[at : at + count, :, :] = total.reshape(count, ROWS, LANES)
        at += count


def face_shapes(planes):
    return [
        jax.ShapeDtypeStruct((2 * REACH * planes, LANES), jnp.float32),
        jax.ShapeDtypeStruct((planes, ROWS, LANES), jnp.float32),
    ]


def pack_kernel(n, *refs):
    pack_into(refs[:n], refs[n], refs[n + 1])


def pack_faces(pieces):
    planes = sum(piece.shape[0] for piece in pieces)
    return pl.pallas_call(
        functools.partial(pack_kernel, len(pieces)),
        out_shape=face_shapes(planes),
        in_specs=[VMEM] * len(pieces),
        out_specs=[VMEM] * 2,
        compiler_params=pltpu.CompilerParams(vmem_limit_bytes=VMEM_LIMIT),
        cost_estimate=COST,
        name="pack_faces",
    )(*pieces)


def entry_kernel(source_ref, low_ref, y_ref, z_ref):
    low_ref[...] = source_ref[0:REACH]
    pack_into([source_ref], y_ref, z_ref)


def entry(source):
    outer = jax.ShapeDtypeStruct((REACH,) + source.shape[1:], jnp.float32)
    return pl.pallas_call(
        entry_kernel,
        out_shape=[outer] + face_shapes(source.shape[0]),
        in_specs=[VMEM],
        out_specs=[VMEM] * 3,
        compiler_params=pltpu.CompilerParams(vmem_limit_bytes=VMEM_LIMIT),
        cost_estimate=COST,
        name="entry",
    )(source)


def stencil_kernel(counts, sections, second, band_ref, *refs):
    n, m = len(counts), len(sections)
    pieces, y_refs, z_refs = refs[:n], refs[n : n + m], refs[n + m : n + 2 * m]
    potential_ref, weights_ref, halo_ref = refs[n + 2 * m : n + 2 * m + 3]
    rest = list(refs[n + 2 * m + 3 :])
    planes, rows = sum(counts), pieces[0].shape[1]
    source_ref = rest.pop(0) if second else None
    extended, gathered = rest[-2:]
    outputs = rest[:-2]
    face_of = [(y_refs[i], 2 * REACH * q) for i, size in enumerate(sections) for q in range(size)]

    def one_group(group, carry):
        start = pl.multiple_of(group * ROWS, 8)
        before = pl.ds(pl.multiple_of(jnp.maximum(start - 8, 0), 8), 8)
        after = pl.ds(pl.multiple_of(jnp.minimum(start + ROWS, rows - 8), 8), 8)
        at = 0
        for piece, count in zip(pieces, counts):
            here = slice(at, at + count)
            extended[here, 8 : 8 + ROWS, :] = piece[:, pl.ds(start, ROWS), :]
            extended[here, 0:8, :] = piece[:, before, :]
            extended[here, 8 + ROWS : 16 + ROWS, :] = piece[:, after, :]
            at += count

        @pl.when(group == 0)
        def _():
            for p, (face, base) in enumerate(face_of):
                extended[p, 8 - REACH : 8, :] = face[base + REACH : base + 2 * REACH, :]

        @pl.when(group == rows // ROWS - 1)
        def _():
            for p, (face, base) in enumerate(face_of):
                extended[p, 8 + ROWS : 8 + ROWS + REACH, :] = face[base : base + REACH, :]

        own_high, own_low = split(extended[:, 8 : 8 + ROWS, :].reshape(planes * ROWS, LANES))
        packed = jnp.concatenate([z[...] for z in z_refs], axis=0).reshape(planes * ROWS, LANES)
        face_high, face_low = split(pltpu.roll(packed, (LANES - SLOT * group) % LANES, 1))
        both_high = jnp.concatenate([own_high, face_high], axis=1)
        both_low = jnp.concatenate([own_low, face_low], axis=1)
        weights = weights_ref[...]
        along_z = jnp.dot(both_high, weights, preferred_element_type=jnp.float32)
        along_z = along_z[:, :LANES] + along_z[:, LANES:]
        along_z += jnp.dot(both_low, weights[:, :LANES], preferred_element_type=jnp.float32)
        gathered[...] = along_z.reshape(planes, ROWS, LANES)
        for tile in range(ROWS // 8):
            top = 8 + 8 * tile
            within = slice(8 * tile, 8 * tile + 8)
            there = pl.ds(pl.multiple_of(start + 8 * tile, 8), 8)
            own = [extended[p, top : top + 8, :] for p in range(planes)]
            for p in range(planes):
                total = gathered[p, within, :]
                total += (CENTER + potential_ref[p, there, :] * (1.0 / 7.0)) * own[p]
                for k in range(1, REACH + 1):
                    beside = extended[p, top + k : top + k + 8, :] + extended[p, top - k : top - k + 8, :]
                    if p - k >= 0:
                        beside = beside + own[p - k]
                    elif not second:
                        beside = beside + halo_ref[REACH + p - k, there, :]
                    if p + k < planes:
                        beside = beside + own[p + k]
                    elif second:
                        beside = beside + halo_ref[p + k - planes, there, :]
                    total = total + SIDE[k] * beside
                if second:
                    total = 2.0 * total - source_ref[p, there, :]
                    if p < REACH:
                        outputs[5][p, there, :] = total
                    else:
                        outputs[0][p, there, :] = total
                else:
                    at = 0
                    for target in outputs:
                        if at <= p < at + target.shape[0]:
                            target[p - at, there, :] = total
                        at += target.shape[0]
        return carry

    lax.fori_loop(0, rows // ROWS, one_group, 0)
    if second:
        part = rows // 4
        for slot in range(4):
            there = pl.ds(pl.multiple_of((band_ref[0] ^ slot) * part, 8), part)
            outputs[1 + slot][...] = outputs[0][REACH:planes, there, :]


def apply_stencil(pieces, faces, potential, halo, band, source=None):
    second = source is not None
    counts = [piece.shape[0] for piece in pieces]
    planes, rows = sum(counts), pieces[0].shape[1]
    sections = [z.shape[0] for _, z in faces]
    operands = list(pieces) + [y for y, _ in faces] + [z for _, z in faces]
    operands += [potential, jnp.asarray(z_matrix()), halo]
    if second:
        operands.append(source)
        shapes = [(planes, rows, LANES)] + [(planes - REACH, rows // 4, LANES)] * 4
        shapes.append((REACH, rows, LANES))
    else:
        shapes = [(REACH, rows, LANES), (planes - 2 * REACH, rows, LANES), (REACH, rows, LANES)]
    return pl.pallas_call(
        functools.partial(stencil_kernel, counts, sections, second),
        out_shape=[jax.ShapeDtypeStruct(shape, jnp.float32) for shape in shapes],
        in_specs=[SMEM] + [VMEM] * len(operands),
        out_specs=[VMEM] * len(shapes),
        scratch_shapes=[
            pltpu.VMEM((planes, ROWS + 16, LANES), jnp.float32),
            pltpu.VMEM((planes, ROWS, LANES), jnp.float32),
        ],
        compiler_params=pltpu.CompilerParams(vmem_limit_bytes=VMEM_LIMIT),
        cost_estimate=COST,
        name="second_step" if second else "first_step",
    )(band, *operands)


def add_halo(out_ref, partial_ref, halo_ref, high_side, factor):
    rows = halo_ref.shape[1]

    def body(tile, carry):
        there = pl.ds(pl.multiple_of(tile * 8, 8), 8)
        halo = [halo_ref[m, there, :] for m in range(REACH)]
        for j in range(REACH):
            total = partial_ref[j, there, :]
            for k in range(1, REACH + 1):
                m = j + k - REACH if high_side else REACH + j - k
                if 0 <= m < REACH:
                    total = total + (factor * SIDE[k]) * halo[m]
            out_ref[j, there, :] = total
        return carry

    lax.fori_loop(0, rows // 8, body, 0)


def finish_first_kernel(partial_ref, halo_ref, out_ref, y_ref, z_ref):
    add_halo(out_ref, partial_ref, halo_ref, True, 1.0)
    pack_into([out_ref], y_ref, z_ref)


def finish_first(partial, halo):
    planes = partial.shape[0]
    return pl.pallas_call(
        finish_first_kernel,
        out_shape=[jax.ShapeDtypeStruct(partial.shape, jnp.float32)] + face_shapes(planes),
        in_specs=[VMEM] * 2,
        out_specs=[VMEM] * 3,
        compiler_params=pltpu.CompilerParams(vmem_limit_bytes=VMEM_LIMIT),
        cost_estimate=COST,
        name="finish_first",
    )(partial, halo)


def finish_filtered_kernel(band_ref, partial_ref, halo_ref, whole_ref, out_ref, *rest):
    slots, done, semaphore = rest[:4], rest[4], rest[5]
    add_halo(done, partial_ref, halo_ref, False, 2.0)
    copy = pltpu.make_async_copy(done, out_ref.at[0:REACH], semaphore)
    copy.start()
    part = slots[0].shape[1]
    for slot in range(4):
        there = pl.ds(pl.multiple_of((band_ref[0] ^ slot) * part, 8), part)
        slots[slot][...] = done[:, there, :]
    copy.wait()


def finish_filtered(partial, halo, whole, band):
    part = jax.ShapeDtypeStruct((REACH, partial.shape[1] // 4, LANES), jnp.float32)
    return pl.pallas_call(
        finish_filtered_kernel,
        out_shape=[jax.ShapeDtypeStruct(whole.shape, jnp.float32)] + [part] * 4,
        in_specs=[SMEM, VMEM, VMEM, ANY],
        out_specs=[ANY] + [VMEM] * 4,
        input_output_aliases={3: 0},
        scratch_shapes=[pltpu.VMEM(partial.shape, jnp.float32), pltpu.SemaphoreType.DMA(())],
        compiler_params=pltpu.CompilerParams(vmem_limit_bytes=VMEM_LIMIT),
        cost_estimate=COST,
        name="finish_filtered",
    )(band, partial, halo, whole)


PAIRS = [(i, j) for i in range(4) for j in range(i, 4)]


def add_products(refs, totals):
    planes, rows = refs[0].shape[0], refs[0].shape[1]

    def body(p, carried):
        carried = list(carried)
        for tile in range(rows // 8):
            values = [ref[p, 8 * tile : 8 * tile + 8, :] for ref in refs]
            for n, (i, j) in enumerate(PAIRS):
                carried[n] = carried[n] + values[i] * values[j]
        return tuple(carried)

    return lax.fori_loop(0, planes, body, tuple(totals))


def early_gram_kernel(*refs):
    out_ref = refs[-1]
    totals = add_products(refs[:4], [jnp.zeros((8, LANES), jnp.float32)] * len(PAIRS))
    for n in range(len(PAIRS)):
        out_ref[n] = totals[n]


def early_gram(parts):
    return pl.pallas_call(
        early_gram_kernel,
        out_shape=jax.ShapeDtypeStruct((len(PAIRS), 8, LANES), jnp.float32),
        in_specs=[VMEM] * 4,
        out_specs=VMEM,
        compiler_params=pltpu.CompilerParams(vmem_limit_bytes=VMEM_LIMIT),
        cost_estimate=COST,
        name="early_gram",
    )(*parts)


def late_gram_kernel(band_ref, before_ref, *refs):
    out_ref = refs[-1]
    totals = add_products(refs[:4], [before_ref[n] for n in range(len(PAIRS))])
    band = band_ref[0]
    lane = lax.broadcasted_iota(jnp.int32, (1, LANES), 1)
    row = jnp.zeros((1, LANES), jnp.float32)
    for n, (i, j) in enumerate(PAIRS):
        value = jnp.sum(totals[n])
        first, other = band ^ i, band ^ j
        hit = (lane == 4 * first + other) | (lane == 4 * other + first)
        row = row + jnp.where(hit, value, 0.0)
    out_ref[...] = jnp.broadcast_to(row, out_ref.shape)


def late_gram(before, parts, band, peers):
    return pl.pallas_call(
        late_gram_kernel,
        out_shape=jax.ShapeDtypeStruct((peers, LANES), jnp.float32),
        in_specs=[SMEM] + [VMEM] * 5,
        out_specs=VMEM,
        compiler_params=pltpu.CompilerParams(vmem_limit_bytes=VMEM_LIMIT),
        cost_estimate=COST,
        name="late_gram",
    )(band, before, *parts)


def total_kernel(scale, rows_ref, out_ref):
    row = jnp.sum(rows_ref[...], axis=0, keepdims=True) * scale
    for i in range(4):
        out_ref[i : i + 1, :] = row[:, 4 * i : 4 * i + 4]


def total_gram(rows, cell_count):
    return pl.pallas_call(
        functools.partial(total_kernel, 1.0 / cell_count),
        out_shape=jax.ShapeDtypeStruct((4, 4), jnp.float32),
        in_specs=[VMEM],
        out_specs=VMEM,
        cost_estimate=COST,
        name="total_gram",
    )(rows)


def shifted(array, by):
    peers = lax.axis_size("space")
    return lax.ppermute(array, "space", [(i, (i + by) % peers) for i in range(peers)])


def swapped(array, axis, bit):
    return lax.ppermute(array, axis, [(i, i ^ bit) for i in range(lax.axis_size(axis))])


def swapped_faces(faces):
    y_faces, z_faces = faces
    return swapped(y_faces, "space", 2), swapped(z_faces, "space", 1)


def band_exchange(slots):
    moved = {k: swapped(slots[k], "band", k) for k in (3, 2, 1)}
    return [slots[0], moved[1], moved[2], moved[3]]


def on_device(orbitals, potential):
    source, local_potential = orbitals[0, 0], potential[0]
    band = lax.axis_index("band").astype(jnp.int32).reshape(1)
    below = shifted(source[source.shape[0] - REACH :], 4)
    low_planes, *faces = entry(source)
    faces = swapped_faces(faces)
    above = shifted(low_planes, -4)
    low, middle, top = apply_stencil([source], [faces], local_potential, below, band)
    above_first = shifted(low, -4)
    main_faces = swapped_faces(pack_faces([low, middle]))
    top, *top_faces = finish_first(top, above)
    below_first = shifted(top, 4)
    top_faces = swapped_faces(top_faces)
    filtered, *slots, low_filtered = apply_stencil(
        [low, middle, top], [main_faces, top_faces], local_potential, above_first, band, source
    )
    early = early_gram(band_exchange(slots))
    filtered, *slots = finish_filtered(low_filtered, below_first, filtered, band)
    both = ("band", "space")
    rows = late_gram(early, band_exchange(slots), band, lax.axis_size(both))
    everyone = lax.all_to_all(rows, both, 0, 0, tiled=True)
    correlation = total_gram(everyone, filtered.size * lax.axis_size("space"))
    return filtered[None, None], correlation


def solution(mesh):
    placed = (P("band", "space", None, None, None), P("space", None, None, None))
    return jax.shard_map(
        on_device,
        mesh=mesh,
        in_specs=placed,
        out_specs=(P("band", "space", None, None, None), P()),
        check_vma=False,
    )
```

```python
import functools
import math

import jax
import jax.numpy as jnp
from jax import lax
from jax.experimental import pallas as pl
from jax.experimental.pallas import tpu as pltpu
from jax.sharding import PartitionSpec as P

REACH = 6
ROWS = 24
LANES = 128
VMEM_LIMIT = 12 << 20
VMEM = pl.BlockSpec(memory_space=pltpu.VMEM)
SMEM = pl.BlockSpec(memory_space=pltpu.SMEM)
ANY = pl.BlockSpec(memory_space=pl.ANY)
HBM = pl.BlockSpec(memory_space=pltpu.HBM)
COST = pl.CostEstimate(flops=1, bytes_accessed=1, transcendentals=0)
SLOT = 16


def stencil_weights():
    weights = []
    for offset in range(1, 7):
        value = (
            2.0
            * (-1.0) ** (offset + 1)
            * math.factorial(6) ** 2
            / (offset * offset * math.factorial(6 - offset) * math.factorial(6 + offset))
        )
        weights.append(value)
    return [-2.0 * sum(weights)] + weights


WEIGHTS = stencil_weights()
CENTER = (-1.5 * WEIGHTS[0] - 9.0) / 7.0
SIDE = [0.0] + [-0.5 * w / 7.0 for w in WEIGHTS[1:]]


def z_matrix():
    row = lax.broadcasted_iota(jnp.int32, (LANES, LANES), 0)
    column = lax.broadcasted_iota(jnp.int32, (LANES, LANES), 1)
    position = jnp.where(row < REACH, LANES + row, row - 2 * REACH)
    own = jnp.zeros((LANES, LANES), jnp.float32)
    face = own
    for k in range(1, REACH + 1):
        own = jnp.where(jnp.abs(row - column) == k, SIDE[k], own)
        face = jnp.where((row < 2 * REACH) & (jnp.abs(position - column) == k), SIDE[k], face)
    return jnp.concatenate(split(jnp.concatenate([own, face], axis=0)), axis=1)


def selection(group):
    lane = lax.broadcasted_iota(jnp.int32, (LANES, LANES), 0)
    slot = lax.broadcasted_iota(jnp.int32, (LANES, LANES), 1) - SLOT * group
    low = (slot >= 0) & (slot < REACH) & (lane == slot)
    high = (slot >= REACH) & (slot < 2 * REACH) & (lane == slot + (LANES - 2 * REACH))
    chosen = jnp.where(low | high, 1.0, 0.0).astype(jnp.bfloat16)
    return jnp.concatenate([chosen, chosen], axis=0)


def split(values):
    high = values.astype(jnp.bfloat16)
    low = (values - high.astype(jnp.float32)).astype(jnp.bfloat16)
    return high, low


def pack_into(pieces, y_ref, z_ref):
    at = 0
    for piece in pieces:
        count, rows = piece.shape[0], piece.shape[1]
        for p in range(count):
            base = 2 * REACH * (at + p)
            y_ref[base : base + REACH, :] = piece[p, 0:REACH, :]
            y_ref[base + REACH : base + 2 * REACH, :] = piece[p, rows - REACH : rows, :]
        total = None
        for group in range(rows // ROWS):
            block = piece[:, group * ROWS : (group + 1) * ROWS, :].reshape(count * ROWS, LANES)
            high, low = split(block)
            part = jnp.dot(
                jnp.concatenate([high, low], axis=1),
                selection(group),
                preferred_element_type=jnp.float32,
            )
            total = part if total is None else total + part
        z_ref[at : at + count, :, :] = total.reshape(count, ROWS, LANES)
        at += count


def face_shapes(planes):
    return [
        jax.ShapeDtypeStruct((2 * REACH * planes, LANES), jnp.float32),
        jax.ShapeDtypeStruct((planes, ROWS, LANES), jnp.float32),
    ]


def entry_kernel(source_ref, low_ref, y_ref, z_ref):
    low_ref[...] = source_ref[0:REACH]
    pack_into([source_ref], y_ref, z_ref)


def entry(source):
    outer = jax.ShapeDtypeStruct((REACH,) + source.shape[1:], jnp.float32)
    return pl.pallas_call(
        entry_kernel,
        out_shape=[outer] + face_shapes(source.shape[0]),
        in_specs=[VMEM],
        out_specs=[VMEM] * 3,
        compiler_params=pltpu.CompilerParams(vmem_limit_bytes=VMEM_LIMIT),
        cost_estimate=COST,
        name="entry",
    )(source)


def stencil_kernel(counts, sections, second, band_ref, *refs):
    n, m = len(counts), len(sections)
    pieces, y_refs, z_refs = refs[:n], refs[n : n + m], refs[n + m : n + 2 * m]
    potential_ref, halo_ref = refs[n + 2 * m : n + 2 * m + 2]
    rest = list(refs[n + 2 * m + 2 :])
    planes, rows = sum(counts), pieces[0].shape[1]
    source_ref = rest.pop(0) if second else None
    extended, gathered, weights_ref = rest[-3:]
    outputs = rest[:-3]
    weights_ref[...] = z_matrix()
    face_of = [(y_refs[i], 2 * REACH * q) for i, size in enumerate(sections) for q in range(size)]

    def one_group(group, carry):
        start = pl.multiple_of(group * ROWS, 8)
        before = pl.ds(pl.multiple_of(jnp.maximum(start - 8, 0), 8), 8)
        after = pl.ds(pl.multiple_of(jnp.minimum(start + ROWS, rows - 8), 8), 8)
        at = 0
        for piece, count in zip(pieces, counts):
            here = slice(at, at + count)
            extended[here, 8 : 8 + ROWS, :] = piece[:, pl.ds(start, ROWS), :]
            extended[here, 0:8, :] = piece[:, before, :]
            extended[here, 8 + ROWS : 16 + ROWS, :] = piece[:, after, :]
            at += count

        @pl.when(group == 0)
        def _():
            for p, (face, base) in enumerate(face_of):
                extended[p, 8 - REACH : 8, :] = face[base + REACH : base + 2 * REACH, :]

        @pl.when(group == rows // ROWS - 1)
        def _():
            for p, (face, base) in enumerate(face_of):
                extended[p, 8 + ROWS : 8 + ROWS + REACH, :] = face[base : base + REACH, :]

        own_high, own_low = split(extended[:, 8 : 8 + ROWS, :].reshape(planes * ROWS, LANES))
        packed = jnp.concatenate([z[...] for z in z_refs], axis=0).reshape(planes * ROWS, LANES)
        face_high, face_low = split(pltpu.roll(packed, (LANES - SLOT * group) % LANES, 1))
        both_high = jnp.concatenate([own_high, face_high], axis=1)
        both_low = jnp.concatenate([own_low, face_low], axis=1)
        weights = weights_ref[...]
        along_z = jnp.dot(both_high, weights, preferred_element_type=jnp.float32)
        along_z = along_z[:, :LANES] + along_z[:, LANES:]
        along_z += jnp.dot(both_low, weights[:, :LANES], preferred_element_type=jnp.float32)
        gathered[...] = along_z.reshape(planes, ROWS, LANES)
        for tile in range(ROWS // 8):
            top = 8 + 8 * tile
            within = slice(8 * tile, 8 * tile + 8)
            there = pl.ds(pl.multiple_of(start + 8 * tile, 8), 8)
            own = [extended[p, top : top + 8, :] for p in range(planes)]
            for p in range(planes):
                total = gathered[p, within, :]
                total += (CENTER + potential_ref[p, there, :] * (1.0 / 7.0)) * own[p]
                for k in range(1, REACH + 1):
                    beside = extended[p, top + k : top + k + 8, :] + extended[p, top - k : top - k + 8, :]
                    if p - k >= 0:
                        beside = beside + own[p - k]
                    elif not second:
                        beside = beside + halo_ref[REACH + p - k, there, :]
                    if p + k < planes:
                        beside = beside + own[p + k]
                    elif second:
                        beside = beside + halo_ref[p + k - planes, there, :]
                    total = total + SIDE[k] * beside
                if second:
                    total = 2.0 * total - source_ref[p, there, :]
                    if p < REACH:
                        outputs[5][p, there, :] = total
                    else:
                        outputs[0][p, there, :] = total
                else:
                    at = 0
                    for target in outputs:
                        if at <= p < at + target.shape[0]:
                            target[p - at, there, :] = total
                        at += target.shape[0]
        return carry

    lax.fori_loop(0, rows // ROWS, one_group, 0)
    if second:
        part = rows // 4
        for slot in range(4):
            there = pl.ds(pl.multiple_of((band_ref[0] ^ slot) * part, 8), part)
            outputs[1 + slot][...] = outputs[0][REACH:planes, there, :]


def apply_stencil(pieces, faces, potential, halo, band, source=None):
    second = source is not None
    counts = [piece.shape[0] for piece in pieces]
    planes, rows = sum(counts), pieces[0].shape[1]
    sections = [z.shape[0] for _, z in faces]
    operands = list(pieces) + [y for y, _ in faces] + [z for _, z in faces]
    operands += [potential, halo]
    if second:
        operands.append(source)
        shapes = [(planes, rows, LANES)] + [(planes - REACH, rows // 4, LANES)] * 4
        shapes.append((REACH, rows, LANES))
    else:
        shapes = [(REACH, rows, LANES), (planes - 2 * REACH, rows, LANES), (REACH, rows, LANES)]
    return pl.pallas_call(
        functools.partial(stencil_kernel, counts, sections, second),
        out_shape=[jax.ShapeDtypeStruct(shape, jnp.float32) for shape in shapes],
        in_specs=[SMEM] + [VMEM] * len(operands),
        out_specs=[VMEM] * len(shapes),
        scratch_shapes=[
            pltpu.VMEM((planes, ROWS + 16, LANES), jnp.float32),
            pltpu.VMEM((planes, ROWS, LANES), jnp.float32),
            pltpu.VMEM((2 * LANES, 2 * LANES), jnp.bfloat16),
        ],
        compiler_params=pltpu.CompilerParams(vmem_limit_bytes=VMEM_LIMIT),
        cost_estimate=COST,
        name="second_step" if second else "first_step",
    )(band, *operands)


def add_halo(out_ref, partial_ref, halo_ref, high_side, factor):
    rows = halo_ref.shape[1]

    def body(tile, carry):
        there = pl.ds(pl.multiple_of(tile * 8, 8), 8)
        halo = [halo_ref[m, there, :] for m in range(REACH)]
        for j in range(REACH):
            total = partial_ref[j, there, :]
            for k in range(1, REACH + 1):
                m = j + k - REACH if high_side else REACH + j - k
                if 0 <= m < REACH:
                    total = total + (factor * SIDE[k]) * halo[m]
            out_ref[j, there, :] = total
        return carry

    lax.fori_loop(0, rows // 8, body, 0)


def finish_first_kernel(low_ref, middle_ref, partial_ref, halo_ref, top_ref, y_ref, z_ref):
    add_halo(top_ref, partial_ref, halo_ref, True, 1.0)
    pack_into([low_ref, middle_ref, top_ref], y_ref, z_ref)


def finish_first(low, middle, partial, halo):
    planes = low.shape[0] + middle.shape[0] + partial.shape[0]
    return pl.pallas_call(
        finish_first_kernel,
        out_shape=[jax.ShapeDtypeStruct(partial.shape, jnp.float32)] + face_shapes(planes),
        in_specs=[VMEM] * 4,
        out_specs=[VMEM] * 3,
        compiler_params=pltpu.CompilerParams(vmem_limit_bytes=VMEM_LIMIT),
        cost_estimate=COST,
        name="finish_first",
    )(low, middle, partial, halo)


def finish_filtered_kernel(band_ref, partial_ref, halo_ref, whole_ref, out_ref, *rest):
    slots, done, semaphore = rest[:4], rest[4], rest[5]
    add_halo(done, partial_ref, halo_ref, False, 2.0)
    copy = pltpu.make_async_copy(done, out_ref.at[0:REACH], semaphore)
    copy.start()
    part = slots[0].shape[1]
    for slot in range(4):
        there = pl.ds(pl.multiple_of((band_ref[0] ^ slot) * part, 8), part)
        slots[slot][...] = done[:, there, :]
    copy.wait()


def finish_filtered(partial, halo, whole, band):
    part = jax.ShapeDtypeStruct((REACH, partial.shape[1] // 4, LANES), jnp.float32)
    return pl.pallas_call(
        finish_filtered_kernel,
        out_shape=[jax.ShapeDtypeStruct(whole.shape, jnp.float32)] + [part] * 4,
        in_specs=[SMEM, VMEM, VMEM, ANY],
        out_specs=[ANY] + [VMEM] * 4,
        input_output_aliases={3: 0},
        scratch_shapes=[pltpu.VMEM(partial.shape, jnp.float32), pltpu.SemaphoreType.DMA(())],
        compiler_params=pltpu.CompilerParams(vmem_limit_bytes=VMEM_LIMIT),
        cost_estimate=COST,
        name="finish_filtered",
    )(band, partial, halo, whole)


PAIRS = [(i, j) for i in range(4) for j in range(i, 4)]


def add_products(refs, totals):
    planes, rows = refs[0].shape[0], refs[0].shape[1]

    def body(p, carried):
        carried = list(carried)
        for tile in range(rows // 8):
            values = [ref[p, 8 * tile : 8 * tile + 8, :] for ref in refs]
            for n, (i, j) in enumerate(PAIRS):
                carried[n] = carried[n] + values[i] * values[j]
        return tuple(carried)

    return lax.fori_loop(0, planes, body, tuple(totals))


def early_gram_kernel(*refs):
    out_ref = refs[-1]
    totals = add_products(refs[:4], [jnp.zeros((8, LANES), jnp.float32)] * len(PAIRS))
    for n in range(len(PAIRS)):
        out_ref[n] = totals[n]


def early_gram(parts):
    return pl.pallas_call(
        early_gram_kernel,
        out_shape=jax.ShapeDtypeStruct((len(PAIRS), 8, LANES), jnp.float32),
        in_specs=[VMEM] * 4,
        out_specs=VMEM,
        compiler_params=pltpu.CompilerParams(vmem_limit_bytes=VMEM_LIMIT),
        cost_estimate=COST,
        name="early_gram",
    )(*parts)


def late_gram_kernel(band_ref, before_ref, *refs):
    out_ref = refs[-1]
    totals = add_products(refs[:4], [before_ref[n] for n in range(len(PAIRS))])
    band = band_ref[0]
    lane = lax.broadcasted_iota(jnp.int32, (1, LANES), 1)
    row = jnp.zeros((1, LANES), jnp.float32)
    for n, (i, j) in enumerate(PAIRS):
        value = jnp.sum(totals[n])
        first, other = band ^ i, band ^ j
        hit = (lane == 4 * first + other) | (lane == 4 * other + first)
        row = row + jnp.where(hit, value, 0.0)
    out_ref[...] = jnp.broadcast_to(row, out_ref.shape)


def late_gram(before, parts, band, peers):
    return pl.pallas_call(
        late_gram_kernel,
        out_shape=jax.ShapeDtypeStruct((peers, LANES), jnp.float32),
        in_specs=[SMEM] + [VMEM] * 5,
        out_specs=VMEM,
        compiler_params=pltpu.CompilerParams(vmem_limit_bytes=VMEM_LIMIT),
        cost_estimate=COST,
        name="late_gram",
    )(band, before, *parts)


def shifted(array, by):
    peers = lax.axis_size("space")
    return lax.ppermute(array, "space", [(i, (i + by) % peers) for i in range(peers)])


def swapped(array, axis, bit):
    return lax.ppermute(array, axis, [(i, i ^ bit) for i in range(lax.axis_size(axis))])


def swapped_faces(faces):
    y_faces, z_faces = faces
    return swapped(y_faces, "space", 2), swapped(z_faces, "space", 1)


def band_exchange(slots):
    moved = {k: swapped(slots[k], "band", k) for k in (3, 2, 1)}
    return [slots[0], moved[1], moved[2], moved[3]]


def on_device(orbitals, potential):
    source, local_potential = orbitals[0, 0], potential[0]
    band = lax.axis_index("band").astype(jnp.int32).reshape(1)
    below = shifted(source[source.shape[0] - REACH :], 4)
    low_planes, *faces = entry(source)
    faces = swapped_faces(faces)
    above = shifted(low_planes, -4)
    low, middle, top = apply_stencil([source], [faces], local_potential, below, band)
    above_first = shifted(low, -4)
    top, *faces = finish_first(low, middle, top, above)
    below_first = shifted(top, 4)
    faces = swapped_faces(faces)
    filtered, *slots, low_filtered = apply_stencil(
        [low, middle, top], [faces], local_potential, above_first, band, source
    )
    early = early_gram(band_exchange(slots))
    filtered, *slots = finish_filtered(low_filtered, below_first, filtered, band)
    both = ("band", "space")
    rows = late_gram(early, band_exchange(slots), band, lax.axis_size(both))
    everyone = lax.all_to_all(rows, both, 0, 0, tiled=True)
    summed = jnp.sum(everyone, axis=0)[:16].reshape(4, 4)
    correlation = summed / jnp.float32(filtered.size * lax.axis_size("space"))
    return filtered[None, None], correlation


def solution(mesh):
    placed = (P("band", "space", None, None, None), P("space", None, None, None))
    return jax.shard_map(
        on_device,
        mesh=mesh,
        in_specs=placed,
        out_specs=(P("band", "space", None, None, None), P()),
        check_vma=False,
    )
```

```python
import functools
import math

import jax
import jax.numpy as jnp
from jax import lax
from jax.experimental import pallas as pl
from jax.experimental.pallas import tpu as pltpu
from jax.sharding import PartitionSpec as P

REACH = 6
ROWS = 24
LANES = 128
VMEM_LIMIT = 12 << 20
VMEM = pl.BlockSpec(memory_space=pltpu.VMEM)
SMEM = pl.BlockSpec(memory_space=pltpu.SMEM)
ANY = pl.BlockSpec(memory_space=pl.ANY)
HBM = pl.BlockSpec(memory_space=pltpu.HBM)
COST = pl.CostEstimate(flops=1, bytes_accessed=1, transcendentals=0)
SLOT = 16


def stencil_weights():
    weights = []
    for offset in range(1, 7):
        value = (
            2.0
            * (-1.0) ** (offset + 1)
            * math.factorial(6) ** 2
            / (offset * offset * math.factorial(6 - offset) * math.factorial(6 + offset))
        )
        weights.append(value)
    return [-2.0 * sum(weights)] + weights


WEIGHTS = stencil_weights()
CENTER = (-1.5 * WEIGHTS[0] - 9.0) / 7.0
SIDE = [0.0] + [-0.5 * w / 7.0 for w in WEIGHTS[1:]]


def z_matrix():
    row = lax.broadcasted_iota(jnp.int32, (LANES, LANES), 0)
    column = lax.broadcasted_iota(jnp.int32, (LANES, LANES), 1)
    position = jnp.where(row < REACH, LANES + row, row - 2 * REACH)
    own = jnp.zeros((LANES, LANES), jnp.float32)
    face = own
    for k in range(1, REACH + 1):
        own = jnp.where(jnp.abs(row - column) == k, SIDE[k], own)
        face = jnp.where((row < 2 * REACH) & (jnp.abs(position - column) == k), SIDE[k], face)
    return jnp.concatenate(split(jnp.concatenate([own, face], axis=0)), axis=1)


def selection(group):
    lane = lax.broadcasted_iota(jnp.int32, (LANES, LANES), 0)
    slot = lax.broadcasted_iota(jnp.int32, (LANES, LANES), 1) - SLOT * group
    low = (slot >= 0) & (slot < REACH) & (lane == slot)
    high = (slot >= REACH) & (slot < 2 * REACH) & (lane == slot + (LANES - 2 * REACH))
    chosen = jnp.where(low | high, 1.0, 0.0).astype(jnp.bfloat16)
    return jnp.concatenate([chosen, chosen], axis=0)


def split(values):
    high = values.astype(jnp.bfloat16)
    low = (values - high.astype(jnp.float32)).astype(jnp.bfloat16)
    return high, low


def pack_into(pieces, y_ref, z_ref):
    at = 0
    for piece in pieces:
        count, rows = piece.shape[0], piece.shape[1]
        for p in range(count):
            base = 2 * REACH * (at + p)
            y_ref[base : base + REACH, :] = piece[p, 0:REACH, :]
            y_ref[base + REACH : base + 2 * REACH, :] = piece[p, rows - REACH : rows, :]
        total = None
        for group in range(rows // ROWS):
            block = piece[:, group * ROWS : (group + 1) * ROWS, :].reshape(count * ROWS, LANES)
            high, low = split(block)
            part = jnp.dot(
                jnp.concatenate([high, low], axis=1),
                selection(group),
                preferred_element_type=jnp.float32,
            )
            total = part if total is None else total + part
        z_ref[at : at + count, :, :] = total.reshape(count, ROWS, LANES)
        at += count


def face_shapes(planes):
    return [
        jax.ShapeDtypeStruct((2 * REACH * planes, LANES), jnp.float32),
        jax.ShapeDtypeStruct((planes, ROWS, LANES), jnp.float32),
    ]


def entry_kernel(band_ref, source_ref, low_ref, y_ref, z_ref):
    low_ref[...] = source_ref[0:REACH]
    pack_into([source_ref], y_ref, z_ref)


def entry(band, source):
    outer = jax.ShapeDtypeStruct((REACH,) + source.shape[1:], jnp.float32)
    return pl.pallas_call(
        entry_kernel,
        out_shape=[outer] + face_shapes(source.shape[0]),
        in_specs=[SMEM, VMEM],
        out_specs=[VMEM] * 3,
        compiler_params=pltpu.CompilerParams(vmem_limit_bytes=VMEM_LIMIT),
        cost_estimate=COST,
        name="entry",
    )(band, source)


def stencil_kernel(counts, sections, second, band_ref, *refs):
    n, m = len(counts), len(sections)
    pieces, y_refs, z_refs = refs[:n], refs[n : n + m], refs[n + m : n + 2 * m]
    potential_ref, halo_ref = refs[n + 2 * m : n + 2 * m + 2]
    rest = list(refs[n + 2 * m + 2 :])
    planes, rows = sum(counts), pieces[0].shape[1]
    source_ref = rest.pop(0) if second else None
    extended, gathered, weights_ref = rest[-3:]
    outputs = rest[:-3]
    weights_ref[...] = z_matrix()
    face_of = [(y_refs[i], 2 * REACH * q) for i, size in enumerate(sections) for q in range(size)]

    def one_group(group, carry):
        start = pl.multiple_of(group * ROWS, 8)
        before = pl.ds(pl.multiple_of(jnp.maximum(start - 8, 0), 8), 8)
        after = pl.ds(pl.multiple_of(jnp.minimum(start + ROWS, rows - 8), 8), 8)
        at = 0
        for piece, count in zip(pieces, counts):
            here = slice(at, at + count)
            extended[here, 8 : 8 + ROWS, :] = piece[:, pl.ds(start, ROWS), :]
            extended[here, 0:8, :] = piece[:, before, :]
            extended[here, 8 + ROWS : 16 + ROWS, :] = piece[:, after, :]
            at += count

        @pl.when(group == 0)
        def _():
            for p, (face, base) in enumerate(face_of):
                extended[p, 8 - REACH : 8, :] = face[base + REACH : base + 2 * REACH, :]

        @pl.when(group == rows // ROWS - 1)
        def _():
            for p, (face, base) in enumerate(face_of):
                extended[p, 8 + ROWS : 8 + ROWS + REACH, :] = face[base : base + REACH, :]

        own_high, own_low = split(extended[:, 8 : 8 + ROWS, :].reshape(planes * ROWS, LANES))
        packed = jnp.concatenate([z[...] for z in z_refs], axis=0).reshape(planes * ROWS, LANES)
        face_high, face_low = split(pltpu.roll(packed, (LANES - SLOT * group) % LANES, 1))
        both_high = jnp.concatenate([own_high, face_high], axis=1)
        both_low = jnp.concatenate([own_low, face_low], axis=1)
        weights = weights_ref[...]
        along_z = jnp.dot(both_high, weights, preferred_element_type=jnp.float32)
        along_z = along_z[:, :LANES] + along_z[:, LANES:]
        along_z += jnp.dot(both_low, weights[:, :LANES], preferred_element_type=jnp.float32)
        gathered[...] = along_z.reshape(planes, ROWS, LANES)
        for tile in range(ROWS // 8):
            top = 8 + 8 * tile
            within = slice(8 * tile, 8 * tile + 8)
            there = pl.ds(pl.multiple_of(start + 8 * tile, 8), 8)
            own = [extended[p, top : top + 8, :] for p in range(planes)]
            for p in range(planes):
                total = gathered[p, within, :]
                total += (CENTER + potential_ref[p, there, :] * (1.0 / 7.0)) * own[p]
                for k in range(1, REACH + 1):
                    beside = extended[p, top + k : top + k + 8, :] + extended[p, top - k : top - k + 8, :]
                    if p - k >= 0:
                        beside = beside + own[p - k]
                    elif not second:
                        beside = beside + halo_ref[REACH + p - k, there, :]
                    if p + k < planes:
                        beside = beside + own[p + k]
                    elif second:
                        beside = beside + halo_ref[p + k - planes, there, :]
                    total = total + SIDE[k] * beside
                if second:
                    total = 2.0 * total - source_ref[p, there, :]
                    if p < REACH:
                        outputs[5][p, there, :] = total
                    else:
                        outputs[0][p, there, :] = total
                else:
                    at = 0
                    for target in outputs:
                        if at <= p < at + target.shape[0]:
                            target[p - at, there, :] = total
                        at += target.shape[0]
        return carry

    lax.fori_loop(0, rows // ROWS, one_group, 0)
    if second:
        part = rows // 4
        for slot in range(4):
            there = pl.ds(pl.multiple_of((band_ref[0] ^ slot) * part, 8), part)
            outputs[1 + slot][...] = outputs[0][REACH:planes, there, :]


def apply_stencil(pieces, faces, potential, halo, band, source=None):
    second = source is not None
    counts = [piece.shape[0] for piece in pieces]
    planes, rows = sum(counts), pieces[0].shape[1]
    sections = [z.shape[0] for _, z in faces]
    operands = list(pieces) + [y for y, _ in faces] + [z for _, z in faces]
    operands += [potential, halo]
    if second:
        operands.append(source)
        shapes = [(planes, rows, LANES)] + [(planes - REACH, rows // 4, LANES)] * 4
        shapes.append((REACH, rows, LANES))
    else:
        shapes = [(REACH, rows, LANES), (planes - 2 * REACH, rows, LANES), (REACH, rows, LANES)]
    return pl.pallas_call(
        functools.partial(stencil_kernel, counts, sections, second),
        out_shape=[jax.ShapeDtypeStruct(shape, jnp.float32) for shape in shapes],
        in_specs=[SMEM] + [VMEM] * len(operands),
        out_specs=[VMEM] * len(shapes),
        scratch_shapes=[
            pltpu.VMEM((planes, ROWS + 16, LANES), jnp.float32),
            pltpu.VMEM((planes, ROWS, LANES), jnp.float32),
            pltpu.VMEM((2 * LANES, 2 * LANES), jnp.bfloat16),
        ],
        compiler_params=pltpu.CompilerParams(vmem_limit_bytes=VMEM_LIMIT),
        cost_estimate=COST,
        name="second_step" if second else "first_step",
    )(band, *operands)


def add_halo(out_ref, partial_ref, halo_ref, high_side, factor):
    rows = halo_ref.shape[1]

    def body(tile, carry):
        there = pl.ds(pl.multiple_of(tile * 8, 8), 8)
        halo = [halo_ref[m, there, :] for m in range(REACH)]
        for j in range(REACH):
            total = partial_ref[j, there, :]
            for k in range(1, REACH + 1):
                m = j + k - REACH if high_side else REACH + j - k
                if 0 <= m < REACH:
                    total = total + (factor * SIDE[k]) * halo[m]
            out_ref[j, there, :] = total
        return carry

    lax.fori_loop(0, rows // 8, body, 0)


def finish_first_kernel(low_ref, middle_ref, partial_ref, halo_ref, top_ref, y_ref, z_ref):
    add_halo(top_ref, partial_ref, halo_ref, True, 1.0)
    pack_into([low_ref, middle_ref, top_ref], y_ref, z_ref)


def finish_first(low, middle, partial, halo):
    planes = low.shape[0] + middle.shape[0] + partial.shape[0]
    return pl.pallas_call(
        finish_first_kernel,
        out_shape=[jax.ShapeDtypeStruct(partial.shape, jnp.float32)] + face_shapes(planes),
        in_specs=[VMEM] * 4,
        out_specs=[VMEM] * 3,
        compiler_params=pltpu.CompilerParams(vmem_limit_bytes=VMEM_LIMIT),
        cost_estimate=COST,
        name="finish_first",
    )(low, middle, partial, halo)


def finish_filtered_kernel(band_ref, partial_ref, halo_ref, whole_ref, out_ref, *rest):
    slots, done, semaphore = rest[:4], rest[4], rest[5]
    add_halo(done, partial_ref, halo_ref, False, 2.0)
    copy = pltpu.make_async_copy(done, out_ref.at[0:REACH], semaphore)
    copy.start()
    part = slots[0].shape[1]
    for slot in range(4):
        there = pl.ds(pl.multiple_of((band_ref[0] ^ slot) * part, 8), part)
        slots[slot][...] = done[:, there, :]
    copy.wait()


def finish_filtered(partial, halo, whole, band):
    part = jax.ShapeDtypeStruct((REACH, partial.shape[1] // 4, LANES), jnp.float32)
    return pl.pallas_call(
        finish_filtered_kernel,
        out_shape=[jax.ShapeDtypeStruct(whole.shape, jnp.float32)] + [part] * 4,
        in_specs=[SMEM, VMEM, VMEM, ANY],
        out_specs=[ANY] + [VMEM] * 4,
        input_output_aliases={3: 0},
        scratch_shapes=[pltpu.VMEM(partial.shape, jnp.float32), pltpu.SemaphoreType.DMA(())],
        compiler_params=pltpu.CompilerParams(vmem_limit_bytes=VMEM_LIMIT),
        cost_estimate=COST,
        name="finish_filtered",
    )(band, partial, halo, whole)


PAIRS = [(i, j) for i in range(4) for j in range(i, 4)]


def add_products(refs, totals):
    planes, rows = refs[0].shape[0], refs[0].shape[1]

    def body(p, carried):
        carried = list(carried)
        for tile in range(rows // 8):
            values = [ref[p, 8 * tile : 8 * tile + 8, :] for ref in refs]
            for n, (i, j) in enumerate(PAIRS):
                carried[n] = carried[n] + values[i] * values[j]
        return tuple(carried)

    return lax.fori_loop(0, planes, body, tuple(totals))


def early_gram_kernel(*refs):
    out_ref = refs[-1]
    totals = add_products(refs[:4], [jnp.zeros((8, LANES), jnp.float32)] * len(PAIRS))
    for n in range(len(PAIRS)):
        out_ref[n] = totals[n]


def early_gram(parts):
    return pl.pallas_call(
        early_gram_kernel,
        out_shape=jax.ShapeDtypeStruct((len(PAIRS), 8, LANES), jnp.float32),
        in_specs=[VMEM] * 4,
        out_specs=VMEM,
        compiler_params=pltpu.CompilerParams(vmem_limit_bytes=VMEM_LIMIT),
        cost_estimate=COST,
        name="early_gram",
    )(*parts)


def late_gram_kernel(band_ref, before_ref, *refs):
    out_ref = refs[-1]
    totals = add_products(refs[:4], [before_ref[n] for n in range(len(PAIRS))])
    band = band_ref[0]
    lane = lax.broadcasted_iota(jnp.int32, (1, LANES), 1)
    row = jnp.zeros((1, LANES), jnp.float32)
    for n, (i, j) in enumerate(PAIRS):
        value = jnp.sum(totals[n])
        first, other = band ^ i, band ^ j
        hit = (lane == 4 * first + other) | (lane == 4 * other + first)
        row = row + jnp.where(hit, value, 0.0)
    out_ref[...] = jnp.broadcast_to(row, out_ref.shape)


def late_gram(before, parts, band, peers):
    return pl.pallas_call(
        late_gram_kernel,
        out_shape=jax.ShapeDtypeStruct((peers, LANES), jnp.float32),
        in_specs=[SMEM] + [VMEM] * 5,
        out_specs=VMEM,
        compiler_params=pltpu.CompilerParams(vmem_limit_bytes=VMEM_LIMIT),
        cost_estimate=COST,
        name="late_gram",
    )(band, before, *parts)


def shifted(array, by):
    peers = lax.axis_size("space")
    return lax.ppermute(array, "space", [(i, (i + by) % peers) for i in range(peers)])


def swapped(array, axis, bit):
    return lax.ppermute(array, axis, [(i, i ^ bit) for i in range(lax.axis_size(axis))])


def swapped_faces(faces):
    y_faces, z_faces = faces
    return swapped(y_faces, "space", 2), swapped(z_faces, "space", 1)


def band_exchange(slots):
    moved = {k: swapped(slots[k], "band", k) for k in (3, 2, 1)}
    return [slots[0], moved[1], moved[2], moved[3]]


def on_device(orbitals, potential):
    source, local_potential = orbitals[0, 0], potential[0]
    band = lax.axis_index("band").astype(jnp.int32).reshape(1)
    below = shifted(source[source.shape[0] - REACH :], 4)
    low_planes, *faces = entry(band, source)
    faces = swapped_faces(faces)
    above = shifted(low_planes, -4)
    low, middle, top = apply_stencil([source], [faces], local_potential, below, band)
    above_first = shifted(low, -4)
    top, *faces = finish_first(low, middle, top, above)
    below_first = shifted(top, 4)
    faces = swapped_faces(faces)
    filtered, *slots, low_filtered = apply_stencil(
        [low, middle, top], [faces], local_potential, above_first, band, source
    )
    early = early_gram(band_exchange(slots))
    filtered, *slots = finish_filtered(low_filtered, below_first, filtered, band)
    both = ("band", "space")
    rows = late_gram(early, band_exchange(slots), band, lax.axis_size(both))
    everyone = lax.all_to_all(rows, both, 0, 0, tiled=True)
    summed = jnp.sum(everyone, axis=0)[:16].reshape(4, 4)
    correlation = summed / jnp.float32(filtered.size * lax.axis_size("space"))
    return filtered[None, None], correlation


def solution(mesh):
    placed = (P("band", "space", None, None, None), P("space", None, None, None))
    return jax.shard_map(
        on_device,
        mesh=mesh,
        in_specs=placed,
        out_specs=(P("band", "space", None, None, None), P()),
        check_vma=False,
    )
```

```python
import functools
import math

import jax
import jax.numpy as jnp
from jax import lax
from jax.experimental import pallas as pl
from jax.experimental.pallas import tpu as pltpu
from jax.sharding import PartitionSpec as P

REACH = 6
ROWS = 24
LANES = 128
VMEM_LIMIT = 12 << 20
VMEM = pl.BlockSpec(memory_space=pltpu.VMEM)
SMEM = pl.BlockSpec(memory_space=pltpu.SMEM)
ANY = pl.BlockSpec(memory_space=pl.ANY)
HBM = pl.BlockSpec(memory_space=pltpu.HBM)
COST = pl.CostEstimate(flops=1, bytes_accessed=1, transcendentals=0)
SLOT = 16


def stencil_weights():
    weights = []
    for offset in range(1, 7):
        value = (
            2.0
            * (-1.0) ** (offset + 1)
            * math.factorial(6) ** 2
            / (offset * offset * math.factorial(6 - offset) * math.factorial(6 + offset))
        )
        weights.append(value)
    return [-2.0 * sum(weights)] + weights


WEIGHTS = stencil_weights()
CENTER = (-1.5 * WEIGHTS[0] - 9.0) / 7.0
SIDE = [0.0] + [-0.5 * w / 7.0 for w in WEIGHTS[1:]]


def z_matrix():
    row = lax.broadcasted_iota(jnp.int32, (LANES, LANES), 0)
    column = lax.broadcasted_iota(jnp.int32, (LANES, LANES), 1)
    position = jnp.where(row < REACH, LANES + row, row - 2 * REACH)
    own = jnp.zeros((LANES, LANES), jnp.float32)
    face = own
    for k in range(1, REACH + 1):
        own = jnp.where(jnp.abs(row - column) == k, SIDE[k], own)
        face = jnp.where((row < 2 * REACH) & (jnp.abs(position - column) == k), SIDE[k], face)
    return jnp.concatenate(split(jnp.concatenate([own, face], axis=0)), axis=1)


def selection(group):
    lane = lax.broadcasted_iota(jnp.int32, (LANES, LANES), 0)
    slot = lax.broadcasted_iota(jnp.int32, (LANES, LANES), 1) - SLOT * group
    low = (slot >= 0) & (slot < REACH) & (lane == slot)
    high = (slot >= REACH) & (slot < 2 * REACH) & (lane == slot + (LANES - 2 * REACH))
    chosen = jnp.where(low | high, 1.0, 0.0).astype(jnp.bfloat16)
    return jnp.concatenate([chosen, chosen], axis=0)


def split(values):
    high = values.astype(jnp.bfloat16)
    low = (values - high.astype(jnp.float32)).astype(jnp.bfloat16)
    return high, low


def pack_into(pieces, y_ref, z_ref):
    at = 0
    for piece in pieces:
        count, rows = piece.shape[0], piece.shape[1]
        for p in range(count):
            base = 2 * REACH * (at + p)
            y_ref[base : base + REACH, :] = piece[p, 0:8, :][0:REACH]
            y_ref[base + REACH : base + 2 * REACH, :] = piece[p, rows - 8 : rows, :][8 - REACH : 8]
        total = None
        for group in range(rows // ROWS):
            block = piece[:, group * ROWS : (group + 1) * ROWS, :].reshape(count * ROWS, LANES)
            high, low = split(block)
            part = jnp.dot(
                jnp.concatenate([high, low], axis=1),
                selection(group),
                preferred_element_type=jnp.float32,
            )
            total = part if total is None else total + part
        z_ref[at : at + count, :, :] = total.reshape(count, ROWS, LANES)
        at += count


def face_shapes(planes):
    return [
        jax.ShapeDtypeStruct((2 * REACH * planes + 8, LANES), jnp.float32),
        jax.ShapeDtypeStruct((planes, ROWS, LANES), jnp.float32),
    ]


def entry_kernel(band_ref, source_ref, low_ref, y_ref, z_ref):
    low_ref[...] = source_ref[0:REACH]
    pack_into([source_ref], y_ref, z_ref)


def entry(band, source):
    outer = jax.ShapeDtypeStruct((REACH,) + source.shape[1:], jnp.float32)
    return pl.pallas_call(
        entry_kernel,
        out_shape=[outer] + face_shapes(source.shape[0]),
        in_specs=[SMEM, VMEM],
        out_specs=[VMEM] * 3,
        compiler_params=pltpu.CompilerParams(vmem_limit_bytes=VMEM_LIMIT),
        cost_estimate=COST,
        name="entry",
    )(band, source)


def stencil_kernel(counts, sections, second, band_ref, *refs):
    n, m = len(counts), len(sections)
    pieces, y_refs, z_refs = refs[:n], refs[n : n + m], refs[n + m : n + 2 * m]
    potential_ref, halo_ref = refs[n + 2 * m : n + 2 * m + 2]
    rest = list(refs[n + 2 * m + 2 :])
    planes, rows = sum(counts), pieces[0].shape[1]
    source_ref = rest.pop(0) if second else None
    extended, gathered, weights_ref = rest[-3:]
    outputs = rest[:-3]
    weights_ref[...] = z_matrix()
    face_of = [(y_refs[i], 2 * REACH * q) for i, size in enumerate(sections) for q in range(size)]

    def one_group(group, carry):
        start = pl.multiple_of(group * ROWS, 8)
        before = pl.ds(pl.multiple_of(jnp.maximum(start - 8, 0), 8), 8)
        after = pl.ds(pl.multiple_of(jnp.minimum(start + ROWS, rows - 8), 8), 8)
        at = 0
        for piece, count in zip(pieces, counts):
            here = slice(at, at + count)
            extended[here, 8 : 8 + ROWS, :] = piece[:, pl.ds(start, ROWS), :]
            extended[here, 0:8, :] = piece[:, before, :]
            extended[here, 8 + ROWS : 16 + ROWS, :] = piece[:, after, :]
            at += count

        @pl.when(group == 0)
        def _():
            for p, (face, base) in enumerate(face_of):
                extended[p, 0:8, :] = face[base + 2 * REACH - 8 : base + 2 * REACH, :]

        @pl.when(group == rows // ROWS - 1)
        def _():
            for p, (face, base) in enumerate(face_of):
                extended[p, 8 + ROWS : 16 + ROWS, :] = face[base : base + 8, :]

        own_high, own_low = split(extended[:, 8 : 8 + ROWS, :].reshape(planes * ROWS, LANES))
        packed = jnp.concatenate([z[...] for z in z_refs], axis=0).reshape(planes * ROWS, LANES)
        face_high, face_low = split(pltpu.roll(packed, (LANES - SLOT * group) % LANES, 1))
        both_high = jnp.concatenate([own_high, face_high], axis=1)
        both_low = jnp.concatenate([own_low, face_low], axis=1)
        weights = weights_ref[...]
        along_z = jnp.dot(both_high, weights, preferred_element_type=jnp.float32)
        along_z = along_z[:, :LANES] + along_z[:, LANES:]
        along_z += jnp.dot(both_low, weights[:, :LANES], preferred_element_type=jnp.float32)
        gathered[...] = along_z.reshape(planes, ROWS, LANES)
        for tile in range(ROWS // 8):
            top = 8 + 8 * tile
            within = slice(8 * tile, 8 * tile + 8)
            there = pl.ds(pl.multiple_of(start + 8 * tile, 8), 8)
            own = [extended[p, top : top + 8, :] for p in range(planes)]
            for p in range(planes):
                total = gathered[p, within, :]
                total += (CENTER + potential_ref[p, there, :] * (1.0 / 7.0)) * own[p]
                for k in range(1, REACH + 1):
                    beside = extended[p, top + k : top + k + 8, :] + extended[p, top - k : top - k + 8, :]
                    if p - k >= 0:
                        beside = beside + own[p - k]
                    elif not second:
                        beside = beside + halo_ref[REACH + p - k, there, :]
                    if p + k < planes:
                        beside = beside + own[p + k]
                    elif second:
                        beside = beside + halo_ref[p + k - planes, there, :]
                    total = total + SIDE[k] * beside
                if second:
                    total = 2.0 * total - source_ref[p, there, :]
                    if p < REACH:
                        outputs[5][p, there, :] = total
                    else:
                        outputs[0][p, there, :] = total
                else:
                    at = 0
                    for target in outputs:
                        if at <= p < at + target.shape[0]:
                            target[p - at, there, :] = total
                        at += target.shape[0]
        return carry

    lax.fori_loop(0, rows // ROWS, one_group, 0)
    if second:
        part = rows // 4
        for slot in range(4):
            there = pl.ds(pl.multiple_of((band_ref[0] ^ slot) * part, 8), part)
            outputs[1 + slot][...] = outputs[0][REACH:planes, there, :]


def apply_stencil(pieces, faces, potential, halo, band, source=None):
    second = source is not None
    counts = [piece.shape[0] for piece in pieces]
    planes, rows = sum(counts), pieces[0].shape[1]
    sections = [z.shape[0] for _, z in faces]
    operands = list(pieces) + [y for y, _ in faces] + [z for _, z in faces]
    operands += [potential, halo]
    if second:
        operands.append(source)
        shapes = [(planes, rows, LANES)] + [(planes - REACH, rows // 4, LANES)] * 4
        shapes.append((REACH, rows, LANES))
    else:
        shapes = [(REACH, rows, LANES), (planes - 2 * REACH, rows, LANES), (REACH, rows, LANES)]
    return pl.pallas_call(
        functools.partial(stencil_kernel, counts, sections, second),
        out_shape=[jax.ShapeDtypeStruct(shape, jnp.float32) for shape in shapes],
        in_specs=[SMEM] + [VMEM] * len(operands),
        out_specs=[VMEM] * len(shapes),
        scratch_shapes=[
            pltpu.VMEM((planes, ROWS + 16, LANES), jnp.float32),
            pltpu.VMEM((planes, ROWS, LANES), jnp.float32),
            pltpu.VMEM((2 * LANES, 2 * LANES), jnp.bfloat16),
        ],
        compiler_params=pltpu.CompilerParams(vmem_limit_bytes=VMEM_LIMIT),
        cost_estimate=COST,
        name="second_step" if second else "first_step",
    )(band, *operands)


def add_halo(out_ref, partial_ref, halo_ref, high_side, factor):
    rows = halo_ref.shape[1]

    def body(tile, carry):
        there = pl.ds(pl.multiple_of(tile * 8, 8), 8)
        halo = [halo_ref[m, there, :] for m in range(REACH)]
        for j in range(REACH):
            total = partial_ref[j, there, :]
            for k in range(1, REACH + 1):
                m = j + k - REACH if high_side else REACH + j - k
                if 0 <= m < REACH:
                    total = total + (factor * SIDE[k]) * halo[m]
            out_ref[j, there, :] = total
        return carry

    lax.fori_loop(0, rows // 8, body, 0)


def finish_first_kernel(low_ref, middle_ref, partial_ref, halo_ref, top_ref, y_ref, z_ref):
    add_halo(top_ref, partial_ref, halo_ref, True, 1.0)
    pack_into([low_ref, middle_ref, top_ref], y_ref, z_ref)


def finish_first(low, middle, partial, halo):
    planes = low.shape[0] + middle.shape[0] + partial.shape[0]
    return pl.pallas_call(
        finish_first_kernel,
        out_shape=[jax.ShapeDtypeStruct(partial.shape, jnp.float32)] + face_shapes(planes),
        in_specs=[VMEM] * 4,
        out_specs=[VMEM] * 3,
        compiler_params=pltpu.CompilerParams(vmem_limit_bytes=VMEM_LIMIT),
        cost_estimate=COST,
        name="finish_first",
    )(low, middle, partial, halo)


def finish_filtered_kernel(band_ref, partial_ref, halo_ref, whole_ref, out_ref, *rest):
    slots, done, semaphore = rest[:4], rest[4], rest[5]
    add_halo(done, partial_ref, halo_ref, False, 2.0)
    copy = pltpu.make_async_copy(done, out_ref.at[0:REACH], semaphore)
    copy.start()
    part = slots[0].shape[1]
    for slot in range(4):
        there = pl.ds(pl.multiple_of((band_ref[0] ^ slot) * part, 8), part)
        slots[slot][...] = done[:, there, :]
    copy.wait()


def finish_filtered(partial, halo, whole, band):
    part = jax.ShapeDtypeStruct((REACH, partial.shape[1] // 4, LANES), jnp.float32)
    return pl.pallas_call(
        finish_filtered_kernel,
        out_shape=[jax.ShapeDtypeStruct(whole.shape, jnp.float32)] + [part] * 4,
        in_specs=[SMEM, VMEM, VMEM, ANY],
        out_specs=[ANY] + [VMEM] * 4,
        input_output_aliases={3: 0},
        scratch_shapes=[pltpu.VMEM(partial.shape, jnp.float32), pltpu.SemaphoreType.DMA(())],
        compiler_params=pltpu.CompilerParams(vmem_limit_bytes=VMEM_LIMIT),
        cost_estimate=COST,
        name="finish_filtered",
    )(band, partial, halo, whole)


PAIRS = [(i, j) for i in range(4) for j in range(i, 4)]


def add_products(refs, totals):
    planes, rows = refs[0].shape[0], refs[0].shape[1]

    def body(p, carried):
        carried = list(carried)
        for tile in range(rows // 8):
            values = [ref[p, 8 * tile : 8 * tile + 8, :] for ref in refs]
            for n, (i, j) in enumerate(PAIRS):
                carried[n] = carried[n] + values[i] * values[j]
        return tuple(carried)

    return lax.fori_loop(0, planes, body, tuple(totals))


def early_gram_kernel(*refs):
    out_ref = refs[-1]
    totals = add_products(refs[:4], [jnp.zeros((8, LANES), jnp.float32)] * len(PAIRS))
    for n in range(len(PAIRS)):
        out_ref[n] = totals[n]


def early_gram(parts):
    return pl.pallas_call(
        early_gram_kernel,
        out_shape=jax.ShapeDtypeStruct((len(PAIRS), 8, LANES), jnp.float32),
        in_specs=[VMEM] * 4,
        out_specs=VMEM,
        compiler_params=pltpu.CompilerParams(vmem_limit_bytes=VMEM_LIMIT),
        cost_estimate=COST,
        name="early_gram",
    )(*parts)


def late_gram_kernel(band_ref, before_ref, *refs):
    out_ref = refs[-1]
    totals = add_products(refs[:4], [before_ref[n] for n in range(len(PAIRS))])
    band = band_ref[0]
    lane = lax.broadcasted_iota(jnp.int32, (1, LANES), 1)
    row = jnp.zeros((1, LANES), jnp.float32)
    for n, (i, j) in enumerate(PAIRS):
        value = jnp.sum(totals[n])
        first, other = band ^ i, band ^ j
        hit = (lane == 4 * first + other) | (lane == 4 * other + first)
        row = row + jnp.where(hit, value, 0.0)
    out_ref[...] = jnp.broadcast_to(row, out_ref.shape)


def late_gram(before, parts, band, peers):
    return pl.pallas_call(
        late_gram_kernel,
        out_shape=jax.ShapeDtypeStruct((peers, LANES), jnp.float32),
        in_specs=[SMEM] + [VMEM] * 5,
        out_specs=VMEM,
        compiler_params=pltpu.CompilerParams(vmem_limit_bytes=VMEM_LIMIT),
        cost_estimate=COST,
        name="late_gram",
    )(band, before, *parts)


def shifted(array, by):
    peers = lax.axis_size("space")
    return lax.ppermute(array, "space", [(i, (i + by) % peers) for i in range(peers)])


def swapped(array, axis, bit):
    return lax.ppermute(array, axis, [(i, i ^ bit) for i in range(lax.axis_size(axis))])


def swapped_faces(faces):
    y_faces, z_faces = faces
    return swapped(y_faces, "space", 2), swapped(z_faces, "space", 1)


def band_exchange(slots):
    moved = {k: swapped(slots[k], "band", k) for k in (3, 2, 1)}
    return [slots[0], moved[1], moved[2], moved[3]]


def on_device(orbitals, potential):
    source, local_potential = orbitals[0, 0], potential[0]
    band = lax.axis_index("band").astype(jnp.int32).reshape(1)
    below = shifted(source[source.shape[0] - REACH :], 4)
    low_planes, *faces = entry(band, source)
    faces = swapped_faces(faces)
    above = shifted(low_planes, -4)
    low, middle, top = apply_stencil([source], [faces], local_potential, below, band)
    above_first = shifted(low, -4)
    top, *faces = finish_first(low, middle, top, above)
    below_first = shifted(top, 4)
    faces = swapped_faces(faces)
    filtered, *slots, low_filtered = apply_stencil(
        [low, middle, top], [faces], local_potential, above_first, band, source
    )
    early = early_gram(band_exchange(slots))
    filtered, *slots = finish_filtered(low_filtered, below_first, filtered, band)
    both = ("band", "space")
    rows = late_gram(early, band_exchange(slots), band, lax.axis_size(both))
    everyone = lax.all_to_all(rows, both, 0, 0, tiled=True)
    summed = jnp.sum(everyone, axis=0)[:16].reshape(4, 4)
    correlation = summed / jnp.float32(filtered.size * lax.axis_size("space"))
    return filtered[None, None], correlation


def solution(mesh):
    placed = (P("band", "space", None, None, None), P("space", None, None, None))
    return jax.shard_map(
        on_device,
        mesh=mesh,
        in_specs=placed,
        out_specs=(P("band", "space", None, None, None), P()),
        check_vma=False,
    )
```

```python
import functools
import math

import jax
import jax.numpy as jnp
from jax import lax
from jax.experimental import pallas as pl
from jax.experimental.pallas import tpu as pltpu
from jax.sharding import PartitionSpec as P

REACH = 6
ROWS = 24
LANES = 128
VMEM_LIMIT = 12 << 20
VMEM = pl.BlockSpec(memory_space=pltpu.VMEM)
ANY = pl.BlockSpec(memory_space=pl.ANY)
HBM = pl.BlockSpec(memory_space=pltpu.HBM)
COST = pl.CostEstimate(flops=1, bytes_accessed=1, transcendentals=0)
SLOT = 16


def stencil_weights():
    weights = []
    for offset in range(1, 7):
        value = (
            2.0
            * (-1.0) ** (offset + 1)
            * math.factorial(6) ** 2
            / (offset * offset * math.factorial(6 - offset) * math.factorial(6 + offset))
        )
        weights.append(value)
    return [-2.0 * sum(weights)] + weights


WEIGHTS = stencil_weights()
CENTER = (-1.5 * WEIGHTS[0] - 9.0) / 7.0
SIDE = [0.0] + [-0.5 * w / 7.0 for w in WEIGHTS[1:]]


def z_matrix():
    row = lax.broadcasted_iota(jnp.int32, (LANES, LANES), 0)
    column = lax.broadcasted_iota(jnp.int32, (LANES, LANES), 1)
    position = jnp.where(row < REACH, LANES + row, row - 2 * REACH)
    own = jnp.zeros((LANES, LANES), jnp.float32)
    face = own
    for k in range(1, REACH + 1):
        own = jnp.where(jnp.abs(row - column) == k, SIDE[k], own)
        face = jnp.where((row < 2 * REACH) & (jnp.abs(position - column) == k), SIDE[k], face)
    return jnp.concatenate(split(jnp.concatenate([own, face], axis=0)), axis=1)


def selection(group):
    lane = lax.broadcasted_iota(jnp.int32, (LANES, LANES), 0)
    slot = lax.broadcasted_iota(jnp.int32, (LANES, LANES), 1) - SLOT * group
    low = (slot >= 0) & (slot < REACH) & (lane == slot)
    high = (slot >= REACH) & (slot < 2 * REACH) & (lane == slot + (LANES - 2 * REACH))
    chosen = jnp.where(low | high, 1.0, 0.0).astype(jnp.bfloat16)
    return jnp.concatenate([chosen, chosen], axis=0)


def split(values):
    high = values.astype(jnp.bfloat16)
    low = (values - high.astype(jnp.float32)).astype(jnp.bfloat16)
    return high, low


def pack_into(pieces, y_ref, z_ref):
    at = 0
    for piece in pieces:
        count, rows = piece.shape[0], piece.shape[1]
        for p in range(count):
            base = 2 * REACH * (at + p)
            y_ref[base : base + REACH, :] = piece[p, 0:8, :][0:REACH]
            y_ref[base + REACH : base + 2 * REACH, :] = piece[p, rows - 8 : rows, :][8 - REACH : 8]
        total = None
        for group in range(rows // ROWS):
            block = piece[:, group * ROWS : (group + 1) * ROWS, :].reshape(count * ROWS, LANES)
            high, low = split(block)
            part = jnp.dot(
                jnp.concatenate([high, low], axis=1),
                selection(group),
                preferred_element_type=jnp.float32,
            )
            total = part if total is None else total + part
        z_ref[at : at + count, :, :] = total.reshape(count, ROWS, LANES)
        at += count


def face_shapes(planes):
    return [
        jax.ShapeDtypeStruct((2 * REACH * planes + 8, LANES), jnp.float32),
        jax.ShapeDtypeStruct((planes, ROWS, LANES), jnp.float32),
    ]


def entry_kernel(sent_ref, source_ref, low_ref, y_ref, z_ref):
    low_ref[...] = source_ref[0:REACH]
    pack_into([source_ref], y_ref, z_ref)


def entry(sent, source):
    outer = jax.ShapeDtypeStruct((REACH,) + source.shape[1:], jnp.float32)
    return pl.pallas_call(
        entry_kernel,
        out_shape=[outer] + face_shapes(source.shape[0]),
        in_specs=[ANY, VMEM],
        out_specs=[VMEM] * 3,
        compiler_params=pltpu.CompilerParams(vmem_limit_bytes=VMEM_LIMIT),
        cost_estimate=COST,
        name="entry",
    )(sent, source)


def stencil_kernel(counts, sections, second, *refs):
    n, m = len(counts), len(sections)
    pieces, y_refs, z_refs = refs[:n], refs[n : n + m], refs[n + m : n + 2 * m]
    potential_ref, halo_ref = refs[n + 2 * m : n + 2 * m + 2]
    rest = list(refs[n + 2 * m + 2 :])
    planes, rows = sum(counts), pieces[0].shape[1]
    source_ref = rest.pop(0) if second else None
    extended, gathered, weights_ref = rest[-3:]
    outputs = rest[:-3]
    weights_ref[...] = z_matrix()
    face_of = [(y_refs[i], 2 * REACH * q) for i, size in enumerate(sections) for q in range(size)]

    def one_group(group, carry):
        start = pl.multiple_of(group * ROWS, 8)
        before = pl.ds(pl.multiple_of(jnp.maximum(start - 8, 0), 8), 8)
        after = pl.ds(pl.multiple_of(jnp.minimum(start + ROWS, rows - 8), 8), 8)
        at = 0
        for piece, count in zip(pieces, counts):
            here = slice(at, at + count)
            extended[here, 8 : 8 + ROWS, :] = piece[:, pl.ds(start, ROWS), :]
            extended[here, 0:8, :] = piece[:, before, :]
            extended[here, 8 + ROWS : 16 + ROWS, :] = piece[:, after, :]
            at += count

        @pl.when(group == 0)
        def _():
            for p, (face, base) in enumerate(face_of):
                extended[p, 0:8, :] = face[base + 2 * REACH - 8 : base + 2 * REACH, :]

        @pl.when(group == rows // ROWS - 1)
        def _():
            for p, (face, base) in enumerate(face_of):
                extended[p, 8 + ROWS : 16 + ROWS, :] = face[base : base + 8, :]

        own_high, own_low = split(extended[:, 8 : 8 + ROWS, :].reshape(planes * ROWS, LANES))
        packed = jnp.concatenate([z[...] for z in z_refs], axis=0).reshape(planes * ROWS, LANES)
        face_high, face_low = split(pltpu.roll(packed, (LANES - SLOT * group) % LANES, 1))
        both_high = jnp.concatenate([own_high, face_high], axis=1)
        both_low = jnp.concatenate([own_low, face_low], axis=1)
        weights = weights_ref[...]
        along_z = jnp.dot(both_high, weights, preferred_element_type=jnp.float32)
        along_z = along_z[:, :LANES] + along_z[:, LANES:]
        along_z += jnp.dot(both_low, weights[:, :LANES], preferred_element_type=jnp.float32)
        gathered[...] = along_z.reshape(planes, ROWS, LANES)
        for tile in range(ROWS // 8):
            top = 8 + 8 * tile
            within = slice(8 * tile, 8 * tile + 8)
            there = pl.ds(pl.multiple_of(start + 8 * tile, 8), 8)
            own = [extended[p, top : top + 8, :] for p in range(planes)]
            for p in range(planes):
                total = gathered[p, within, :]
                total += (CENTER + potential_ref[p, there, :] * (1.0 / 7.0)) * own[p]
                for k in range(1, REACH + 1):
                    beside = extended[p, top + k : top + k + 8, :] + extended[p, top - k : top - k + 8, :]
                    if p - k >= 0:
                        beside = beside + own[p - k]
                    elif not second:
                        beside = beside + halo_ref[REACH + p - k, there, :]
                    if p + k < planes:
                        beside = beside + own[p + k]
                    elif second:
                        beside = beside + halo_ref[p + k - planes, there, :]
                    total = total + SIDE[k] * beside
                if second:
                    total = 2.0 * total - source_ref[p, there, :]
                    if p < REACH:
                        outputs[5][p, there, :] = total
                    else:
                        outputs[0][p, there, :] = total
                else:
                    at = 0
                    for target in outputs:
                        if at <= p < at + target.shape[0]:
                            target[p - at, there, :] = total
                        at += target.shape[0]
        return carry

    lax.fori_loop(0, rows // ROWS, one_group, 0)
    if second:
        part = rows // 4
        for slot in range(4):
            there = pl.ds(pl.multiple_of((lax.axis_index("band") ^ slot) * part, 8), part)
            outputs[1 + slot][...] = outputs[0][REACH:planes, there, :]


def apply_stencil(pieces, faces, potential, halo, source=None):
    second = source is not None
    counts = [piece.shape[0] for piece in pieces]
    planes, rows = sum(counts), pieces[0].shape[1]
    sections = [z.shape[0] for _, z in faces]
    operands = list(pieces) + [y for y, _ in faces] + [z for _, z in faces]
    operands += [potential, halo]
    if second:
        operands.append(source)
        shapes = [(planes, rows, LANES)] + [(planes - REACH, rows // 4, LANES)] * 4
        shapes.append((REACH, rows, LANES))
    else:
        shapes = [(REACH, rows, LANES), (planes - 2 * REACH, rows, LANES), (REACH, rows, LANES)]
    return pl.pallas_call(
        functools.partial(stencil_kernel, counts, sections, second),
        out_shape=[jax.ShapeDtypeStruct(shape, jnp.float32) for shape in shapes],
        in_specs=[VMEM] * len(operands),
        out_specs=[VMEM] * len(shapes),
        scratch_shapes=[
            pltpu.VMEM((planes, ROWS + 16, LANES), jnp.float32),
            pltpu.VMEM((planes, ROWS, LANES), jnp.float32),
            pltpu.VMEM((2 * LANES, 2 * LANES), jnp.bfloat16),
        ],
        compiler_params=pltpu.CompilerParams(vmem_limit_bytes=VMEM_LIMIT),
        cost_estimate=COST,
        name="second_step" if second else "first_step",
    )(*operands)


def add_halo(out_ref, partial_ref, halo_ref, high_side, factor):
    rows = halo_ref.shape[1]

    def body(tile, carry):
        there = pl.ds(pl.multiple_of(tile * 8, 8), 8)
        halo = [halo_ref[m, there, :] for m in range(REACH)]
        for j in range(REACH):
            total = partial_ref[j, there, :]
            for k in range(1, REACH + 1):
                m = j + k - REACH if high_side else REACH + j - k
                if 0 <= m < REACH:
                    total = total + (factor * SIDE[k]) * halo[m]
            out_ref[j, there, :] = total
        return carry

    lax.fori_loop(0, rows // 8, body, 0)


def finish_first_kernel(low_ref, middle_ref, partial_ref, halo_ref, top_ref, y_ref, z_ref):
    add_halo(top_ref, partial_ref, halo_ref, True, 1.0)
    pack_into([low_ref, middle_ref, top_ref], y_ref, z_ref)


def finish_first(low, middle, partial, halo):
    planes = low.shape[0] + middle.shape[0] + partial.shape[0]
    return pl.pallas_call(
        finish_first_kernel,
        out_shape=[jax.ShapeDtypeStruct(partial.shape, jnp.float32)] + face_shapes(planes),
        in_specs=[VMEM] * 4,
        out_specs=[VMEM] * 3,
        compiler_params=pltpu.CompilerParams(vmem_limit_bytes=VMEM_LIMIT),
        cost_estimate=COST,
        name="finish_first",
    )(low, middle, partial, halo)


def finish_filtered_kernel(partial_ref, halo_ref, whole_ref, out_ref, *rest):
    slots, done, semaphore = rest[:4], rest[4], rest[5]
    add_halo(done, partial_ref, halo_ref, False, 2.0)
    copy = pltpu.make_async_copy(done, out_ref.at[0:REACH], semaphore)
    copy.start()
    part = slots[0].shape[1]
    for slot in range(4):
        there = pl.ds(pl.multiple_of((lax.axis_index("band") ^ slot) * part, 8), part)
        slots[slot][...] = done[:, there, :]
    copy.wait()


def finish_filtered(partial, halo, whole):
    part = jax.ShapeDtypeStruct((REACH, partial.shape[1] // 4, LANES), jnp.float32)
    return pl.pallas_call(
        finish_filtered_kernel,
        out_shape=[jax.ShapeDtypeStruct(whole.shape, jnp.float32)] + [part] * 4,
        in_specs=[VMEM, VMEM, ANY],
        out_specs=[ANY] + [VMEM] * 4,
        input_output_aliases={2: 0},
        scratch_shapes=[pltpu.VMEM(partial.shape, jnp.float32), pltpu.SemaphoreType.DMA(())],
        compiler_params=pltpu.CompilerParams(vmem_limit_bytes=VMEM_LIMIT),
        cost_estimate=COST,
        name="finish_filtered",
    )(partial, halo, whole)


PAIRS = [(i, j) for i in range(4) for j in range(i, 4)]


def add_products(refs, totals):
    planes, rows = refs[0].shape[0], refs[0].shape[1]

    def body(p, carried):
        carried = list(carried)
        for tile in range(rows // 8):
            values = [ref[p, 8 * tile : 8 * tile + 8, :] for ref in refs]
            for n, (i, j) in enumerate(PAIRS):
                carried[n] = carried[n] + values[i] * values[j]
        return tuple(carried)

    return lax.fori_loop(0, planes, body, tuple(totals))


def early_gram_kernel(*refs):
    out_ref = refs[-1]
    totals = add_products(refs[:4], [jnp.zeros((8, LANES), jnp.float32)] * len(PAIRS))
    for n in range(len(PAIRS)):
        out_ref[n] = totals[n]


def early_gram(parts):
    return pl.pallas_call(
        early_gram_kernel,
        out_shape=jax.ShapeDtypeStruct((len(PAIRS), 8, LANES), jnp.float32),
        in_specs=[VMEM] * 4,
        out_specs=VMEM,
        compiler_params=pltpu.CompilerParams(vmem_limit_bytes=VMEM_LIMIT),
        cost_estimate=COST,
        name="early_gram",
    )(*parts)


def late_gram_kernel(before_ref, *refs):
    out_ref = refs[-1]
    totals = add_products(refs[:4], [before_ref[n] for n in range(len(PAIRS))])
    band = lax.axis_index("band")
    lane = lax.broadcasted_iota(jnp.int32, (1, LANES), 1)
    row = jnp.zeros((1, LANES), jnp.float32)
    for n, (i, j) in enumerate(PAIRS):
        value = jnp.sum(totals[n])
        first, other = band ^ i, band ^ j
        hit = (lane == 4 * first + other) | (lane == 4 * other + first)
        row = row + jnp.where(hit, value, 0.0)
    out_ref[...] = jnp.broadcast_to(row, out_ref.shape)


def late_gram(before, parts, peers):
    return pl.pallas_call(
        late_gram_kernel,
        out_shape=jax.ShapeDtypeStruct((peers, LANES), jnp.float32),
        in_specs=[VMEM] * 5,
        out_specs=VMEM,
        compiler_params=pltpu.CompilerParams(vmem_limit_bytes=VMEM_LIMIT),
        cost_estimate=COST,
        name="late_gram",
    )(before, *parts)


def shifted(array, by):
    peers = lax.axis_size("space")
    return lax.ppermute(array, "space", [(i, (i + by) % peers) for i in range(peers)])


def swapped(array, axis, bit):
    return lax.ppermute(array, axis, [(i, i ^ bit) for i in range(lax.axis_size(axis))])


def swapped_faces(faces):
    y_faces, z_faces = faces
    return swapped(y_faces, "space", 2), swapped(z_faces, "space", 1)


def band_exchange(slots):
    moved = {k: swapped(slots[k], "band", k) for k in (3, 2, 1)}
    return [slots[0], moved[1], moved[2], moved[3]]


def on_device(orbitals, potential):
    source, local_potential = orbitals[0, 0], potential[0]
    high_planes = source[source.shape[0] - REACH :]
    below = shifted(high_planes, 4)
    low_planes, *faces = entry(high_planes, source)
    faces = swapped_faces(faces)
    above = shifted(low_planes, -4)
    low, middle, top = apply_stencil([source], [faces], local_potential, below)
    above_first = shifted(low, -4)
    top, *faces = finish_first(low, middle, top, above)
    below_first = shifted(top, 4)
    faces = swapped_faces(faces)
    filtered, *slots, low_filtered = apply_stencil(
        [low, middle, top], [faces], local_potential, above_first, source
    )
    early = early_gram(band_exchange(slots))
    filtered, *slots = finish_filtered(low_filtered, below_first, filtered)
    both = ("band", "space")
    rows = late_gram(early, band_exchange(slots), lax.axis_size(both))
    everyone = lax.all_to_all(rows, both, 0, 0, tiled=True)
    summed = jnp.sum(everyone, axis=0)[:16].reshape(4, 4)
    correlation = summed / jnp.float32(filtered.size * lax.axis_size("space"))
    return filtered[None, None], correlation


def solution(mesh):
    placed = (P("band", "space", None, None, None), P("space", None, None, None))
    return jax.shard_map(
        on_device,
        mesh=mesh,
        in_specs=placed,
        out_specs=(P("band", "space", None, None, None), P()),
        check_vma=False,
    )
```

```python
import functools
import math

import jax
import jax.numpy as jnp
from jax import lax
from jax.experimental import pallas as pl
from jax.experimental.pallas import tpu as pltpu
from jax.sharding import PartitionSpec as P

REACH = 6
ROWS = 24
LANES = 128
VMEM_LIMIT = 12 << 20
VMEM = pl.BlockSpec(memory_space=pltpu.VMEM)
ANY = pl.BlockSpec(memory_space=pl.ANY)
HBM = pl.BlockSpec(memory_space=pltpu.HBM)
COST = pl.CostEstimate(flops=1, bytes_accessed=1, transcendentals=0)
SLOT = 16


def stencil_weights():
    weights = []
    for offset in range(1, 7):
        value = (
            2.0
            * (-1.0) ** (offset + 1)
            * math.factorial(6) ** 2
            / (offset * offset * math.factorial(6 - offset) * math.factorial(6 + offset))
        )
        weights.append(value)
    return [-2.0 * sum(weights)] + weights


WEIGHTS = stencil_weights()
CENTER = (-1.5 * WEIGHTS[0] - 9.0) / 7.0
SIDE = [0.0] + [-0.5 * w / 7.0 for w in WEIGHTS[1:]]


def z_matrix():
    row = lax.broadcasted_iota(jnp.int32, (LANES, LANES), 0)
    column = lax.broadcasted_iota(jnp.int32, (LANES, LANES), 1)
    position = jnp.where(row < REACH, LANES + row, row - 2 * REACH)
    own = jnp.zeros((LANES, LANES), jnp.float32)
    face = own
    for k in range(1, REACH + 1):
        own = jnp.where(jnp.abs(row - column) == k, SIDE[k], own)
        face = jnp.where((row < 2 * REACH) & (jnp.abs(position - column) == k), SIDE[k], face)
    return jnp.concatenate(split(jnp.concatenate([own, face], axis=0)), axis=1)


def selection(group):
    lane = lax.broadcasted_iota(jnp.int32, (LANES, LANES), 0)
    slot = lax.broadcasted_iota(jnp.int32, (LANES, LANES), 1) - SLOT * group
    low = (slot >= 0) & (slot < REACH) & (lane == slot)
    high = (slot >= REACH) & (slot < 2 * REACH) & (lane == slot + (LANES - 2 * REACH))
    chosen = jnp.where(low | high, 1.0, 0.0).astype(jnp.bfloat16)
    return jnp.concatenate([chosen, chosen], axis=0)


def split(values):
    high = values.astype(jnp.bfloat16)
    low = (values - high.astype(jnp.float32)).astype(jnp.bfloat16)
    return high, low


def pack_into(pieces, y_ref, z_ref):
    at = 0
    for piece in pieces:
        count, rows = piece.shape[0], piece.shape[1]
        for p in range(count):
            base = 2 * REACH * (at + p)
            y_ref[base : base + REACH, :] = piece[p, 0:8, :][0:REACH]
            y_ref[base + REACH : base + 2 * REACH, :] = piece[p, rows - 8 : rows, :][8 - REACH : 8]
        total = None
        for group in range(rows // ROWS):
            block = piece[:, group * ROWS : (group + 1) * ROWS, :].reshape(count * ROWS, LANES)
            high, low = split(block)
            part = jnp.dot(
                jnp.concatenate([high, low], axis=1),
                selection(group),
                preferred_element_type=jnp.float32,
            )
            total = part if total is None else total + part
        z_ref[at : at + count, :, :] = total.reshape(count, ROWS, LANES)
        at += count


def face_shapes(planes):
    return [
        jax.ShapeDtypeStruct((2 * REACH * planes + 8, LANES), jnp.float32),
        jax.ShapeDtypeStruct((planes, ROWS, LANES), jnp.float32),
    ]


def entry_kernel(sent_ref, source_ref, low_ref, y_ref, z_ref):
    low_ref[...] = source_ref[0:REACH]
    pack_into([source_ref], y_ref, z_ref)


def entry(sent, source):
    outer = jax.ShapeDtypeStruct((REACH,) + source.shape[1:], jnp.float32)
    return pl.pallas_call(
        entry_kernel,
        out_shape=[outer] + face_shapes(source.shape[0]),
        in_specs=[ANY, VMEM],
        out_specs=[VMEM] * 3,
        compiler_params=pltpu.CompilerParams(vmem_limit_bytes=VMEM_LIMIT),
        cost_estimate=COST,
        name="entry",
    )(sent, source)


def stencil_kernel(counts, sections, second, *refs):
    n, m = len(counts), len(sections)
    pieces, y_refs, z_refs = refs[:n], refs[n : n + m], refs[n + m : n + 2 * m]
    potential_ref, halo_ref = refs[n + 2 * m : n + 2 * m + 2]
    rest = list(refs[n + 2 * m + 2 :])
    planes, rows = sum(counts), pieces[0].shape[1]
    source_ref = rest.pop(0) if second else None
    extended, gathered, weights_ref = rest[-3:]
    outputs = rest[:-3]
    weights_ref[...] = z_matrix()
    face_of = [(y_refs[i], 2 * REACH * q) for i, size in enumerate(sections) for q in range(size)]

    def one_group(group, carry):
        start = pl.multiple_of(group * ROWS, 8)
        before = pl.ds(pl.multiple_of(jnp.maximum(start - 8, 0), 8), 8)
        after = pl.ds(pl.multiple_of(jnp.minimum(start + ROWS, rows - 8), 8), 8)
        at = 0
        for piece, count in zip(pieces, counts):
            here = slice(at, at + count)
            extended[here, 8 : 8 + ROWS, :] = piece[:, pl.ds(start, ROWS), :]
            extended[here, 0:8, :] = piece[:, before, :]
            extended[here, 8 + ROWS : 16 + ROWS, :] = piece[:, after, :]
            at += count

        @pl.when(group == 0)
        def _():
            for p, (face, base) in enumerate(face_of):
                extended[p, 0:8, :] = face[base + 2 * REACH - 8 : base + 2 * REACH, :]

        @pl.when(group == rows // ROWS - 1)
        def _():
            for p, (face, base) in enumerate(face_of):
                extended[p, 8 + ROWS : 16 + ROWS, :] = face[base : base + 8, :]

        own_high, own_low = split(extended[:, 8 : 8 + ROWS, :].reshape(planes * ROWS, LANES))
        packed = jnp.concatenate([z[...] for z in z_refs], axis=0).reshape(planes * ROWS, LANES)
        face_high, face_low = split(pltpu.roll(packed, (LANES - SLOT * group) % LANES, 1))
        both_high = jnp.concatenate([own_high, face_high], axis=1)
        both_low = jnp.concatenate([own_low, face_low], axis=1)
        weights = weights_ref[...]
        along_z = jnp.dot(both_high, weights, preferred_element_type=jnp.float32)
        along_z = along_z[:, :LANES] + along_z[:, LANES:]
        along_z += jnp.dot(both_low, weights[:, :LANES], preferred_element_type=jnp.float32)
        gathered[...] = along_z.reshape(planes, ROWS, LANES)
        for tile in range(ROWS // 8):
            top = 8 + 8 * tile
            within = slice(8 * tile, 8 * tile + 8)
            there = pl.ds(pl.multiple_of(start + 8 * tile, 8), 8)
            own = [extended[p, top : top + 8, :] for p in range(planes)]
            for p in range(planes):
                total = gathered[p, within, :]
                total += (CENTER + potential_ref[p, there, :] * (1.0 / 7.0)) * own[p]
                for k in range(1, REACH + 1):
                    beside = extended[p, top + k : top + k + 8, :] + extended[p, top - k : top - k + 8, :]
                    if p - k >= 0:
                        beside = beside + own[p - k]
                    elif not second:
                        beside = beside + halo_ref[REACH + p - k, there, :]
                    if p + k < planes:
                        beside = beside + own[p + k]
                    elif second:
                        beside = beside + halo_ref[p + k - planes, there, :]
                    total = total + SIDE[k] * beside
                if second:
                    total = 2.0 * total - source_ref[p, there, :]
                    if p < REACH:
                        outputs[5][p, there, :] = total
                    else:
                        outputs[0][p, there, :] = total
                else:
                    at = 0
                    for target in outputs:
                        if at <= p < at + target.shape[0]:
                            target[p - at, there, :] = total
                        at += target.shape[0]
        return carry

    lax.fori_loop(0, rows // ROWS, one_group, 0)
    if second:
        part = rows // 4
        for slot in range(4):
            there = pl.ds(pl.multiple_of((lax.axis_index("band") ^ slot) * part, 8), part)
            outputs[1 + slot][...] = outputs[0][REACH:planes, there, :]


def apply_stencil(pieces, faces, potential, halo, source=None):
    second = source is not None
    counts = [piece.shape[0] for piece in pieces]
    planes, rows = sum(counts), pieces[0].shape[1]
    sections = [z.shape[0] for _, z in faces]
    operands = list(pieces) + [y for y, _ in faces] + [z for _, z in faces]
    operands += [potential, halo]
    if second:
        operands.append(source)
        shapes = [(planes, rows, LANES)] + [(planes - REACH, rows // 4, LANES)] * 4
        shapes.append((REACH, rows, LANES))
    else:
        shapes = [(REACH, rows, LANES), (planes - 2 * REACH, rows, LANES), (REACH, rows, LANES)]
    return pl.pallas_call(
        functools.partial(stencil_kernel, counts, sections, second),
        out_shape=[jax.ShapeDtypeStruct(shape, jnp.float32) for shape in shapes],
        in_specs=[VMEM] * len(operands),
        out_specs=[VMEM] * len(shapes),
        scratch_shapes=[
            pltpu.VMEM((planes, ROWS + 16, LANES), jnp.float32),
            pltpu.VMEM((planes, ROWS, LANES), jnp.float32),
            pltpu.VMEM((2 * LANES, 2 * LANES), jnp.bfloat16),
        ],
        compiler_params=pltpu.CompilerParams(vmem_limit_bytes=VMEM_LIMIT),
        cost_estimate=COST,
        name="second_step" if second else "first_step",
    )(*operands)


def add_halo(out_ref, partial_ref, halo_ref, high_side, factor):
    rows = halo_ref.shape[1]

    def body(tile, carry):
        there = pl.ds(pl.multiple_of(tile * 8, 8), 8)
        halo = [halo_ref[m, there, :] for m in range(REACH)]
        for j in range(REACH):
            total = partial_ref[j, there, :]
            for k in range(1, REACH + 1):
                m = j + k - REACH if high_side else REACH + j - k
                if 0 <= m < REACH:
                    total = total + (factor * SIDE[k]) * halo[m]
            out_ref[j, there, :] = total
        return carry

    lax.fori_loop(0, rows // 8, body, 0)


def finish_first_kernel(low_ref, middle_ref, partial_ref, halo_ref, top_ref, y_ref, z_ref):
    add_halo(top_ref, partial_ref, halo_ref, True, 1.0)
    pack_into([low_ref, middle_ref, top_ref], y_ref, z_ref)


def finish_first(low, middle, partial, halo):
    planes = low.shape[0] + middle.shape[0] + partial.shape[0]
    return pl.pallas_call(
        finish_first_kernel,
        out_shape=[jax.ShapeDtypeStruct(partial.shape, jnp.float32)] + face_shapes(planes),
        in_specs=[VMEM] * 4,
        out_specs=[VMEM] * 3,
        compiler_params=pltpu.CompilerParams(vmem_limit_bytes=VMEM_LIMIT),
        cost_estimate=COST,
        name="finish_first",
    )(low, middle, partial, halo)


def finish_filtered_kernel(partial_ref, halo_ref, whole_ref, out_ref, *rest):
    slots, done, semaphore = rest[:4], rest[4], rest[5]
    add_halo(done, partial_ref, halo_ref, False, 2.0)
    copy = pltpu.make_async_copy(done, out_ref.at[0:REACH], semaphore)
    copy.start()
    part = slots[0].shape[1]
    for slot in range(4):
        there = pl.ds(pl.multiple_of((lax.axis_index("band") ^ slot) * part, 8), part)
        slots[slot][...] = done[:, there, :]
    copy.wait()


def finish_filtered(partial, halo, whole):
    part = jax.ShapeDtypeStruct((REACH, partial.shape[1] // 4, LANES), jnp.float32)
    return pl.pallas_call(
        finish_filtered_kernel,
        out_shape=[jax.ShapeDtypeStruct(whole.shape, jnp.float32)] + [part] * 4,
        in_specs=[VMEM, VMEM, ANY],
        out_specs=[ANY] + [VMEM] * 4,
        input_output_aliases={2: 0},
        scratch_shapes=[pltpu.VMEM(partial.shape, jnp.float32), pltpu.SemaphoreType.DMA(())],
        compiler_params=pltpu.CompilerParams(vmem_limit_bytes=VMEM_LIMIT),
        cost_estimate=COST,
        name="finish_filtered",
    )(partial, halo, whole)


PAIRS = [(i, j) for i in range(4) for j in range(i, 4)]


def add_products(refs, totals):
    planes, rows = refs[0].shape[0], refs[0].shape[1]

    def body(p, carried):
        carried = list(carried)
        for tile in range(rows // 8):
            values = [ref[p, 8 * tile : 8 * tile + 8, :] for ref in refs]
            for n, (i, j) in enumerate(PAIRS):
                carried[n] = carried[n] + values[i] * values[j]
        return tuple(carried)

    return lax.fori_loop(0, planes, body, tuple(totals))


def early_gram_kernel(*refs):
    out_ref = refs[-1]
    totals = add_products(refs[:4], [jnp.zeros((8, LANES), jnp.float32)] * len(PAIRS))
    for n in range(len(PAIRS)):
        out_ref[n] = totals[n]


def early_gram(parts):
    return pl.pallas_call(
        early_gram_kernel,
        out_shape=jax.ShapeDtypeStruct((len(PAIRS), 8, LANES), jnp.float32),
        in_specs=[VMEM] * 4,
        out_specs=VMEM,
        compiler_params=pltpu.CompilerParams(vmem_limit_bytes=VMEM_LIMIT),
        cost_estimate=COST,
        name="early_gram",
    )(*parts)


def late_gram_kernel(before_ref, *refs):
    out_ref = refs[-1]
    totals = add_products(refs[:4], [before_ref[n] for n in range(len(PAIRS))])
    band = lax.axis_index("band")
    lane = lax.broadcasted_iota(jnp.int32, (1, LANES), 1)
    row = jnp.zeros((1, LANES), jnp.float32)
    for n, (i, j) in enumerate(PAIRS):
        value = jnp.sum(totals[n])
        first, other = band ^ i, band ^ j
        hit = (lane == 4 * first + other) | (lane == 4 * other + first)
        row = row + jnp.where(hit, value, 0.0)
    out_ref[...] = jnp.broadcast_to(row, out_ref.shape)


def late_gram(before, parts, peers):
    return pl.pallas_call(
        late_gram_kernel,
        out_shape=jax.ShapeDtypeStruct((peers, LANES), jnp.float32),
        in_specs=[VMEM] * 5,
        out_specs=VMEM,
        compiler_params=pltpu.CompilerParams(vmem_limit_bytes=VMEM_LIMIT),
        cost_estimate=COST,
        name="late_gram",
    )(before, *parts)


def shifted(array, by):
    peers = lax.axis_size("space")
    return lax.ppermute(array, "space", [(i, (i + by) % peers) for i in range(peers)])


def swapped(array, axis, bit):
    return lax.ppermute(array, axis, [(i, i ^ bit) for i in range(lax.axis_size(axis))])


def swapped_faces(faces):
    y_faces, z_faces = faces
    return swapped(y_faces, "space", 2), swapped(z_faces, "space", 1)


def band_exchange(slots):
    moved = {k: swapped(slots[k], "band", k) for k in (3, 2, 1)}
    return [slots[0], moved[1], moved[2], moved[3]]


def on_device(orbitals, potential):
    source, local_potential = orbitals[0, 0], potential[0]
    high_planes = source[source.shape[0] - REACH :]
    below = shifted(high_planes, 4)
    low_planes, *faces = entry(high_planes, source)
    faces = swapped_faces(faces)
    above = shifted(low_planes, -4)
    low, middle, top = apply_stencil([source], [faces], local_potential, below)
    above_first = shifted(low, -4)
    top, *faces = finish_first(low, middle, top, above)
    below_first = shifted(top, 4)
    faces = swapped_faces(faces)
    filtered, *slots, low_filtered = apply_stencil(
        [low, middle, top], [faces], local_potential, above_first, source
    )
    early = early_gram(band_exchange(slots))
    filtered, *slots = finish_filtered(low_filtered, below_first, filtered)
    both = ("band", "space")
    rows = late_gram(early, band_exchange(slots), lax.axis_size(both))
    everyone = lax.all_to_all(rows, both, 0, 0, tiled=True)
    row = jnp.sum(everyone, axis=0)
    summed = jnp.stack([row[4 * i : 4 * i + 4] for i in range(4)])
    correlation = summed / jnp.float32(filtered.size * lax.axis_size("space"))
    return filtered[None, None], correlation


def solution(mesh):
    placed = (P("band", "space", None, None, None), P("space", None, None, None))
    return jax.shard_map(
        on_device,
        mesh=mesh,
        in_specs=placed,
        out_specs=(P("band", "space", None, None, None), P()),
        check_vma=False,
    )
```

```python
import functools
import math

import jax
import jax.numpy as jnp
from jax import lax
from jax.experimental import pallas as pl
from jax.experimental.pallas import tpu as pltpu
from jax.sharding import PartitionSpec as P

REACH = 6
ROWS = 24
LANES = 128
VMEM_LIMIT = 12 << 20
VMEM = pl.BlockSpec(memory_space=pltpu.VMEM)
ANY = pl.BlockSpec(memory_space=pl.ANY)
HBM = pl.BlockSpec(memory_space=pltpu.HBM)
COST = pl.CostEstimate(flops=1, bytes_accessed=1, transcendentals=0)
SLOT = 16


def stencil_weights():
    weights = []
    for offset in range(1, 7):
        value = (
            2.0
            * (-1.0) ** (offset + 1)
            * math.factorial(6) ** 2
            / (offset * offset * math.factorial(6 - offset) * math.factorial(6 + offset))
        )
        weights.append(value)
    return [-2.0 * sum(weights)] + weights


WEIGHTS = stencil_weights()
CENTER = (-1.5 * WEIGHTS[0] - 9.0) / 7.0
SIDE = [0.0] + [-0.5 * w / 7.0 for w in WEIGHTS[1:]]


def z_matrix():
    row = lax.broadcasted_iota(jnp.int32, (LANES, LANES), 0)
    column = lax.broadcasted_iota(jnp.int32, (LANES, LANES), 1)
    position = jnp.where(row < REACH, LANES + row, row - 2 * REACH)
    own = jnp.zeros((LANES, LANES), jnp.float32)
    face = own
    for k in range(1, REACH + 1):
        own = jnp.where(jnp.abs(row - column) == k, SIDE[k], own)
        face = jnp.where((row < 2 * REACH) & (jnp.abs(position - column) == k), SIDE[k], face)
    return jnp.concatenate(split(jnp.concatenate([own, face], axis=0)), axis=1)


def selection(group):
    lane = lax.broadcasted_iota(jnp.int32, (LANES, LANES), 0)
    slot = lax.broadcasted_iota(jnp.int32, (LANES, LANES), 1) - SLOT * group
    low = (slot >= 0) & (slot < REACH) & (lane == slot)
    high = (slot >= REACH) & (slot < 2 * REACH) & (lane == slot + (LANES - 2 * REACH))
    chosen = jnp.where(low | high, 1.0, 0.0).astype(jnp.bfloat16)
    return jnp.concatenate([chosen, chosen], axis=0)


def split(values):
    high = values.astype(jnp.bfloat16)
    low = (values - high.astype(jnp.float32)).astype(jnp.bfloat16)
    return high, low


def pack_into(pieces, y_ref, z_ref):
    at = 0
    for piece in pieces:
        count, rows = piece.shape[0], piece.shape[1]
        for p in range(count):
            base = 2 * REACH * (at + p)
            y_ref[base : base + REACH, :] = piece[p, 0:8, :][0:REACH]
            y_ref[base + REACH : base + 2 * REACH, :] = piece[p, rows - 8 : rows, :][8 - REACH : 8]
        total = None
        for group in range(rows // ROWS):
            block = piece[:, group * ROWS : (group + 1) * ROWS, :].reshape(count * ROWS, LANES)
            high, low = split(block)
            part = jnp.dot(
                jnp.concatenate([high, low], axis=1),
                selection(group),
                preferred_element_type=jnp.float32,
            )
            total = part if total is None else total + part
        z_ref[at : at + count, :, :] = total.reshape(count, ROWS, LANES)
        at += count


def face_shapes(planes):
    return [
        jax.ShapeDtypeStruct((2 * REACH * planes + 8, LANES), jnp.float32),
        jax.ShapeDtypeStruct((planes, ROWS, LANES), jnp.float32),
    ]


def entry_kernel(sent_ref, source_ref, low_ref, y_ref, z_ref):
    low_ref[...] = source_ref[0:REACH]
    pack_into([source_ref], y_ref, z_ref)


def entry(sent, source):
    outer = jax.ShapeDtypeStruct((REACH,) + source.shape[1:], jnp.float32)
    return pl.pallas_call(
        entry_kernel,
        out_shape=[outer] + face_shapes(source.shape[0]),
        in_specs=[ANY, VMEM],
        out_specs=[VMEM] * 3,
        compiler_params=pltpu.CompilerParams(vmem_limit_bytes=VMEM_LIMIT),
        cost_estimate=COST,
        name="entry",
    )(sent, source)


def stencil_kernel(counts, sections, second, *refs):
    n, m = len(counts), len(sections)
    pieces, y_refs, z_refs = refs[:n], refs[n : n + m], refs[n + m : n + 2 * m]
    potential_ref, halo_ref = refs[n + 2 * m : n + 2 * m + 2]
    rest = list(refs[n + 2 * m + 2 :])
    planes, rows = sum(counts), pieces[0].shape[1]
    source_ref = rest.pop(0) if second else None
    extended, gathered, weights_ref = rest[-3:]
    outputs = rest[:-3]
    weights_ref[...] = z_matrix()
    face_of = [(y_refs[i], 2 * REACH * q) for i, size in enumerate(sections) for q in range(size)]

    def one_group(group, carry):
        start = pl.multiple_of(group * ROWS, 8)
        before = pl.ds(pl.multiple_of(jnp.maximum(start - 8, 0), 8), 8)
        after = pl.ds(pl.multiple_of(jnp.minimum(start + ROWS, rows - 8), 8), 8)
        at = 0
        for piece, count in zip(pieces, counts):
            here = slice(at, at + count)
            extended[here, 8 : 8 + ROWS, :] = piece[:, pl.ds(start, ROWS), :]
            extended[here, 0:8, :] = piece[:, before, :]
            extended[here, 8 + ROWS : 16 + ROWS, :] = piece[:, after, :]
            at += count

        @pl.when(group == 0)
        def _():
            for p, (face, base) in enumerate(face_of):
                extended[p, 0:8, :] = face[base + 2 * REACH - 8 : base + 2 * REACH, :]

        @pl.when(group == rows // ROWS - 1)
        def _():
            for p, (face, base) in enumerate(face_of):
                extended[p, 8 + ROWS : 16 + ROWS, :] = face[base : base + 8, :]

        own_high, own_low = split(extended[:, 8 : 8 + ROWS, :].reshape(planes * ROWS, LANES))
        packed = jnp.concatenate([z[...] for z in z_refs], axis=0).reshape(planes * ROWS, LANES)
        face_high, face_low = split(pltpu.roll(packed, (LANES - SLOT * group) % LANES, 1))
        both_high = jnp.concatenate([own_high, face_high], axis=1)
        both_low = jnp.concatenate([own_low, face_low], axis=1)
        weights = weights_ref[...]
        along_z = jnp.dot(both_high, weights, preferred_element_type=jnp.float32)
        along_z = along_z[:, :LANES] + along_z[:, LANES:]
        along_z += jnp.dot(both_low, weights[:, :LANES], preferred_element_type=jnp.float32)
        gathered[...] = along_z.reshape(planes, ROWS, LANES)
        for tile in range(ROWS // 8):
            top = 8 + 8 * tile
            within = slice(8 * tile, 8 * tile + 8)
            there = pl.ds(pl.multiple_of(start + 8 * tile, 8), 8)
            own = [extended[p, top : top + 8, :] for p in range(planes)]
            for p in range(planes):
                total = gathered[p, within, :]
                total += (CENTER + potential_ref[p, there, :] * (1.0 / 7.0)) * own[p]
                for k in range(1, REACH + 1):
                    beside = extended[p, top + k : top + k + 8, :] + extended[p, top - k : top - k + 8, :]
                    if p - k >= 0:
                        beside = beside + own[p - k]
                    elif not second:
                        beside = beside + halo_ref[REACH + p - k, there, :]
                    if p + k < planes:
                        beside = beside + own[p + k]
                    elif second:
                        beside = beside + halo_ref[p + k - planes, there, :]
                    total = total + SIDE[k] * beside
                if second:
                    total = 2.0 * total - source_ref[p, there, :]
                    if p < REACH:
                        outputs[5][p, there, :] = total
                    else:
                        outputs[0][p, there, :] = total
                else:
                    at = 0
                    for target in outputs:
                        if at <= p < at + target.shape[0]:
                            target[p - at, there, :] = total
                        at += target.shape[0]
        return carry

    lax.fori_loop(0, rows // ROWS, one_group, 0)
    if second:
        part = rows // 4
        for slot in range(4):
            there = pl.ds(pl.multiple_of((lax.axis_index("band") ^ slot) * part, 8), part)
            outputs[1 + slot][...] = outputs[0][REACH:planes, there, :]


def apply_stencil(pieces, faces, potential, halo, source=None):
    second = source is not None
    counts = [piece.shape[0] for piece in pieces]
    planes, rows = sum(counts), pieces[0].shape[1]
    sections = [z.shape[0] for _, z in faces]
    operands = list(pieces) + [y for y, _ in faces] + [z for _, z in faces]
    operands += [potential, halo]
    if second:
        operands.append(source)
        shapes = [(planes, rows, LANES)] + [(planes - REACH, rows // 4, LANES)] * 4
        shapes.append((REACH, rows, LANES))
    else:
        shapes = [(REACH, rows, LANES), (planes - 2 * REACH, rows, LANES), (REACH, rows, LANES)]
    return pl.pallas_call(
        functools.partial(stencil_kernel, counts, sections, second),
        out_shape=[jax.ShapeDtypeStruct(shape, jnp.float32) for shape in shapes],
        in_specs=[VMEM] * len(operands),
        out_specs=[VMEM] * len(shapes),
        scratch_shapes=[
            pltpu.VMEM((planes, ROWS + 16, LANES), jnp.float32),
            pltpu.VMEM((planes, ROWS, LANES), jnp.float32),
            pltpu.VMEM((2 * LANES, 2 * LANES), jnp.bfloat16),
        ],
        compiler_params=pltpu.CompilerParams(vmem_limit_bytes=VMEM_LIMIT),
        cost_estimate=COST,
        name="second_step" if second else "first_step",
    )(*operands)


def add_halo(out_ref, partial_ref, halo_ref, high_side, factor):
    rows = halo_ref.shape[1]

    def body(tile, carry):
        there = pl.ds(pl.multiple_of(tile * 8, 8), 8)
        halo = [halo_ref[m, there, :] for m in range(REACH)]
        for j in range(REACH):
            total = partial_ref[j, there, :]
            for k in range(1, REACH + 1):
                m = j + k - REACH if high_side else REACH + j - k
                if 0 <= m < REACH:
                    total = total + (factor * SIDE[k]) * halo[m]
            out_ref[j, there, :] = total
        return carry

    lax.fori_loop(0, rows // 8, body, 0)


def finish_first_kernel(low_ref, middle_ref, partial_ref, halo_ref, top_ref, y_ref, z_ref):
    add_halo(top_ref, partial_ref, halo_ref, True, 1.0)
    pack_into([low_ref, middle_ref, top_ref], y_ref, z_ref)


def finish_first(low, middle, partial, halo):
    planes = low.shape[0] + middle.shape[0] + partial.shape[0]
    return pl.pallas_call(
        finish_first_kernel,
        out_shape=[jax.ShapeDtypeStruct(partial.shape, jnp.float32)] + face_shapes(planes),
        in_specs=[VMEM] * 4,
        out_specs=[VMEM] * 3,
        compiler_params=pltpu.CompilerParams(vmem_limit_bytes=VMEM_LIMIT),
        cost_estimate=COST,
        name="finish_first",
    )(low, middle, partial, halo)


def finish_filtered_kernel(partial_ref, halo_ref, whole_ref, out_ref, *rest):
    slots, done, semaphore = rest[:4], rest[4], rest[5]
    add_halo(done, partial_ref, halo_ref, False, 2.0)
    copy = pltpu.make_async_copy(done, out_ref.at[0:REACH], semaphore)
    copy.start()
    part = slots[0].shape[1]
    for slot in range(4):
        there = pl.ds(pl.multiple_of((lax.axis_index("band") ^ slot) * part, 8), part)
        slots[slot][...] = done[:, there, :]
    copy.wait()


def finish_filtered(partial, halo, whole):
    part = jax.ShapeDtypeStruct((REACH, partial.shape[1] // 4, LANES), jnp.float32)
    return pl.pallas_call(
        finish_filtered_kernel,
        out_shape=[jax.ShapeDtypeStruct(whole.shape, jnp.float32)] + [part] * 4,
        in_specs=[VMEM, VMEM, ANY],
        out_specs=[ANY] + [VMEM] * 4,
        input_output_aliases={2: 0},
        scratch_shapes=[pltpu.VMEM(partial.shape, jnp.float32), pltpu.SemaphoreType.DMA(())],
        compiler_params=pltpu.CompilerParams(vmem_limit_bytes=VMEM_LIMIT),
        cost_estimate=COST,
        name="finish_filtered",
    )(partial, halo, whole)


PAIRS = [(i, j) for i in range(4) for j in range(i, 4)]


def add_products(refs, totals):
    planes, rows = refs[0].shape[0], refs[0].shape[1]

    def body(p, carried):
        carried = list(carried)
        for tile in range(rows // 8):
            values = [ref[p, 8 * tile : 8 * tile + 8, :] for ref in refs]
            for n, (i, j) in enumerate(PAIRS):
                carried[n] = carried[n] + values[i] * values[j]
        return tuple(carried)

    return lax.fori_loop(0, planes, body, tuple(totals))


def early_gram_kernel(*refs):
    out_ref = refs[-1]
    totals = add_products(refs[:4], [jnp.zeros((8, LANES), jnp.float32)] * len(PAIRS))
    for n in range(len(PAIRS)):
        out_ref[n] = totals[n]


def early_gram(parts):
    return pl.pallas_call(
        early_gram_kernel,
        out_shape=jax.ShapeDtypeStruct((len(PAIRS), 8, LANES), jnp.float32),
        in_specs=[VMEM] * 4,
        out_specs=VMEM,
        compiler_params=pltpu.CompilerParams(vmem_limit_bytes=VMEM_LIMIT),
        cost_estimate=COST,
        name="early_gram",
    )(*parts)


def late_gram_kernel(before_ref, *refs):
    out_ref = refs[-1]
    totals = add_products(refs[:4], [before_ref[n] for n in range(len(PAIRS))])
    band = lax.axis_index("band")
    lane = lax.broadcasted_iota(jnp.int32, (1, LANES), 1)
    row = jnp.zeros((1, LANES), jnp.float32)
    for n, (i, j) in enumerate(PAIRS):
        value = jnp.sum(totals[n])
        first, other = band ^ i, band ^ j
        hit = (lane == 4 * first + other) | (lane == 4 * other + first)
        row = row + jnp.where(hit, value, 0.0)
    out_ref[...] = jnp.broadcast_to(row, out_ref.shape)


def late_gram(before, parts, peers):
    return pl.pallas_call(
        late_gram_kernel,
        out_shape=jax.ShapeDtypeStruct((peers, LANES), jnp.float32),
        in_specs=[VMEM] * 5,
        out_specs=VMEM,
        compiler_params=pltpu.CompilerParams(vmem_limit_bytes=VMEM_LIMIT),
        cost_estimate=COST,
        name="late_gram",
    )(before, *parts)


def shifted(array, by):
    peers = lax.axis_size("space")
    return lax.ppermute(array, "space", [(i, (i + by) % peers) for i in range(peers)])


def swapped(array, axis, bit):
    return lax.ppermute(array, axis, [(i, i ^ bit) for i in range(lax.axis_size(axis))])


def swapped_faces(faces):
    y_faces, z_faces = faces
    return swapped(y_faces, "space", 2), swapped(z_faces, "space", 1)


def band_exchange(slots):
    moved = {k: swapped(slots[k], "band", k) for k in (3, 2, 1)}
    return [slots[0], moved[1], moved[2], moved[3]]


def on_device(orbitals, potential):
    source, local_potential = orbitals[0, 0], potential[0]
    high_planes = orbitals[:, :, source.shape[0] - REACH :]
    below = shifted(high_planes, 4)[0, 0]
    low_planes, *faces = entry(high_planes, source)
    faces = swapped_faces(faces)
    above = shifted(low_planes, -4)
    low, middle, top = apply_stencil([source], [faces], local_potential, below)
    above_first = shifted(low, -4)
    top, *faces = finish_first(low, middle, top, above)
    below_first = shifted(top, 4)
    faces = swapped_faces(faces)
    filtered, *slots, low_filtered = apply_stencil(
        [low, middle, top], [faces], local_potential, above_first, source
    )
    early = early_gram(band_exchange(slots))
    filtered, *slots = finish_filtered(low_filtered, below_first, filtered)
    both = ("band", "space")
    rows = late_gram(early, band_exchange(slots), lax.axis_size(both))
    everyone = lax.all_to_all(rows, both, 0, 0, tiled=True)
    summed = jnp.sum(everyone, axis=0)[:16].reshape(4, 4)
    correlation = summed / jnp.float32(filtered.size * lax.axis_size("space"))
    return filtered[None, None], correlation


def solution(mesh):
    placed = (P("band", "space", None, None, None), P("space", None, None, None))
    return jax.shard_map(
        on_device,
        mesh=mesh,
        in_specs=placed,
        out_specs=(P("band", "space", None, None, None), P()),
        check_vma=False,
    )
```
